32 devices in a mesh: dp: 4 (over y, x), expert: 8 (over z, core).
Axes of the slice: x: 2, y: 2, z: 4, core: 2. Of those that a mesh axis runs over, the one named last changes fastest.
Arguments:
- tokens: bfloat16 [8, 4, 12, 7168], P('expert', 'dp'), may hold values from -6 to 6
- cotangent: bfloat16 [8, 4, 12, 7168], P('expert', 'dp'), may hold values from -6 to 6
- w_gate: bfloat16 [8, 7168, 1024], P('expert', None, 'dp'), may hold values from -0.0625 to 0.0625
- w_up: bfloat16 [8, 7168, 1024], P('expert', None, 'dp'), may hold values from -0.0625 to 0.0625
- w_down: bfloat16 [8, 1024, 7168], P('expert', 'dp'), may hold values from -0.1875 to 0.1875
- routes: int32 [8, 4, 12, 2], P('expert', 'dp'), may hold values from 0 to 7, all different within a row; in each aligned block of 48 rows (0 to 47, 48 to 95, ..., all dimensions but the last counted through in order) at most 18 rows name the same one
- gates: int32 [8, 4, 12, 2], P('expert', 'dp'), may hold values from 4096 to 65535
- matching: int32 [8], replicated, may hold values from 0 to 7, as said below
Outputs:
- grad_input: bfloat16 [8, 4, 12, 7168], P('expert', 'dp')
- grad_gate: bfloat16 [8, 7168, 1024], P('expert', None, 'dp')
- grad_up: bfloat16 [8, 7168, 1024], P('expert', None, 'dp')
- grad_down: bfloat16 [8, 1024, 7168], P('expert', 'dp')
The draws below stay inside these ranges and needn't reach their ends.
Inputs may be any that keep to these rules, and one draw needn't show every extreme that they name: Each token names 2 different experts. Within routes[c] for any c no expert is named more than 18 times. matching[j] is j, or j + 4 for j below 4, or j - 4 above; matching[matching[j]] = j, and the pair of slot 7 always differs from it.
All inputs are finite; a program needn't handle non-finite values.
Results may differ from the reference program's by a relative error of at most 0.019.
Values may be sent and summed in bfloat16 or wider, within the bound.
A program may use at most 192 MiB of HBM per device.

```python
import math
import jax
import jax.numpy as jnp
import numpy as np
from jax import lax

D = 7168
FF = 1024
TOPK = 2
TOK_DEV = 12
EXPERTS = 8
HIDDEN_DEV = 256
CAPC = 18
N_DP = 4


def draw_matching(key, part):
    half = EXPERTS // 2
    flags = jax.random.randint(key, (half,), 0, 2)
    lower = jnp.arange(half, dtype=jnp.int32)
    flags = jnp.where(lower == half - 1, 1, flags).astype(jnp.int32)
    first = lower + flags * half
    second = lower + half - flags * half
    return jnp.concatenate([first, second]).astype(jnp.int32)


def place_ends(entries, key, smallest, high):
    longest = entries.shape.index(max(entries.shape))
    spots = []
    for shift in (0, 1):
        where = [jax.random.randint(jax.random.fold_in(key, axis), (), 0, length) for axis, length in enumerate(entries.shape)]
        where[longest] = (where[longest] + shift) % entries.shape[longest]
        spots.append(tuple(where))
    return entries.at[spots[0]].set(smallest).at[spots[1]].set(high)


def shard_levels(key, shape, split, least, largest):
    factor_of, own = 1.0, jax.random.fold_in(key, 6)
    for axis_at, parts in split:
        steps = jnp.exp(jax.random.uniform(jax.random.fold_in(own, axis_at), (parts,), jnp.float32, least / len(split), largest / len(split)))
        factor_of = factor_of * jnp.repeat(steps, shape[axis_at] // parts).reshape([-1 if axis == axis_at else 1 for axis in range(len(shape))])
    return factor_of


def routed_block(own_key, own, number, rows, count, top, limit, lean):
    sequence = jax.random.permutation(own_key, count)
    heavy_load, usual = portions_of(count, rows * top, limit, lean, True), portions_of(count, rows * top, limit, lean, False)
    places = jnp.arange(count)

    def named(tallies, turn):
        used = int((tallies > 0).sum())
        fixed = max(1, used // 4)
        moved = fixed + (places - fixed + turn * (used - fixed)) % max(1, count - fixed)
        return jnp.zeros((count,), jnp.int32).at[sequence[jnp.where(places < fixed, places, moved)]].set(jnp.asarray(tallies, jnp.int32))

    tallies = jnp.where(number % 4 == 0, named(heavy_load, number // 4), named(usual, number - number // 4 - 1))
    mixed = jax.random.permutation(jax.random.fold_in(own, 3), count)
    donor, receiver = mixed[0:count // 2 * 2:2], mixed[1:count // 2 * 2:2]
    margin = jnp.minimum(tallies[donor] - 1, limit - tallies[receiver]) // 2
    margin = jnp.where((donor == sequence[0]) | (receiver == sequence[0]) | (tallies[receiver] == 0), 0, jnp.maximum(margin, 0))
    moved = jax.random.randint(jax.random.fold_in(own, 4), (count // 2,), 0, 1 << 20) % (margin + 1)
    tallies = tallies.at[donor].add(-moved).at[receiver].add(moved)
    items = jnp.searchsorted(jnp.cumsum(tallies), jnp.arange(rows * top), side="right").astype(jnp.int32)
    grid = items.reshape(top, rows).T
    grid = grid[jax.random.permutation(jax.random.fold_in(own, 1), rows)]
    turn = jax.random.randint(jax.random.fold_in(own, 2), (rows, 1), 0, top)
    return jnp.take_along_axis(grid, (jnp.arange(top)[None, :] + turn) % top, axis=1)


def portions_of(number_of, total, most, slope, full):
    weights = [(1 << 20) // math.isqrt(standing ** slope) + 1 for standing in range(1, number_of + 1)]
    largest = most if full else min(most, max(-(-total // number_of), total * weights[0] // sum(weights)))
    least = 1 if total - largest >= number_of - 1 else 0
    given, rest = [largest] + [least] * (number_of - 1), total - largest - least * (number_of - 1)
    while rest > 0:
        candidates = [i for i in range(1, number_of) if given[i] < largest] or [i for i in range(1, number_of) if given[i] < most]
        mass, remaining = sum([weights[i] for i in candidates]), rest
        for i in candidates:
            more = min(most - given[i], max(1, remaining * weights[i] // mass), rest)
            given[i] = given[i] + more
            rest = rest - more
    return np.array(given)


def centred(stream_key, shape, scale, most, cuts=(), kind=jnp.bfloat16):
    values = jax.random.normal(stream_key, shape, jnp.float32) * scale
    if len(cuts) > 0:
        values = shard_levels(stream_key, shape, cuts, -0.22, 0.18) * values
    return jnp.clip(values, min=-most, max=most).astype(kind)


def setup_inputs(seed: int = 0) -> dict:
    arg_keys = jax.random.split(jax.random.key(seed), 9)
    tokens = centred(arg_keys[0], (EXPERTS, N_DP, TOK_DEV, D), 1.0, 6.0, ((0, 8), (1, 4)))
    cotangent = centred(arg_keys[1], (EXPERTS, N_DP, TOK_DEV, D), 1.0, 6.0, ((0, 8), (1, 4)))
    w_gate = centred(arg_keys[2], (EXPERTS, D, FF), D ** -0.5, 0.0625, ((0, 8), (2, 4)))
    w_up = centred(arg_keys[3], (EXPERTS, D, FF), D ** -0.5, 0.0625, ((0, 8), (2, 4)))
    w_down = centred(arg_keys[4], (EXPERTS, FF, D), FF ** -0.5, 0.1875, ((0, 8), (1, 4)))
    routes_keys = jax.random.split(jax.random.fold_in(arg_keys[5], 1), EXPERTS * N_DP * TOK_DEV // (N_DP * TOK_DEV))
    routes_turns = jax.random.permutation(jax.random.fold_in(arg_keys[5], 3), EXPERTS * N_DP * TOK_DEV // (N_DP * TOK_DEV))
    routes = jax.vmap(lambda own, number: routed_block(jax.random.fold_in(arg_keys[5], 2), own, number, N_DP * TOK_DEV, EXPERTS, TOPK, CAPC, 2))(routes_keys, routes_turns).reshape((EXPERTS, N_DP, TOK_DEV, TOPK))
    gates = place_ends(jax.random.randint(arg_keys[6], (EXPERTS, N_DP, TOK_DEV, TOPK), 4096, 65536), jax.random.fold_in(arg_keys[6], 1), 4096, 65535).astype(jnp.int32)
    matching = draw_matching(jax.random.fold_in(arg_keys[8], 71), 0)
    return dict(tokens=tokens, cotangent=cotangent, w_gate=w_gate, w_up=w_up, w_down=w_down, routes=routes, gates=gates, matching=matching)


def reference(tokens, cotangent, w_gate, w_up, w_down, routes, gates, matching):
    width = tokens.shape[-1]
    flat_rows = tokens.reshape(-1, width)
    flat_cot = cotangent.reshape(-1, width)
    choice_ids = routes.reshape(-1).astype(jnp.int32)
    pick_count = choice_ids.shape[0]
    expert_iota = jnp.arange(EXPERTS, dtype=jnp.int32)
    onehot = (choice_ids[:, None] == expert_iota[None, :]).astype(jnp.int32)
    ranking = jnp.sum(jnp.cumsum(onehot, axis=0) * onehot, axis=1) - 1
    table = jnp.full((EXPERTS, EXPERTS * CAPC), pick_count, jnp.int32)
    table = table.at[choice_ids, ranking.astype(jnp.int32)].set(jnp.arange(pick_count, dtype=jnp.int32))
    scale = gates.reshape(-1).astype(jnp.float32) / 65536.0
    groups = FF // HIDDEN_DEV

    def per_expert(total, inputs):
        picked, gate_mat, up_mat, down_mat = inputs
        valid = picked < pick_count
        safe = jnp.minimum(picked, pick_count - 1)
        owner_tok = safe // TOPK
        rows_in = jnp.where(valid[:, None], flat_rows[owner_tok], jnp.zeros((), flat_rows.dtype))
        gated = scale[safe][:, None] * flat_cot[owner_tok].astype(jnp.float32)
        rows_cot = jnp.where(valid[:, None], gated, jnp.zeros((), jnp.float32)).astype(jnp.bfloat16)
        gate_act = jnp.dot(rows_in, gate_mat, preferred_element_type=jnp.float32)
        up_act = jnp.dot(rows_in, up_mat, preferred_element_type=jnp.float32)
        sigmoid_gate = jax.nn.sigmoid(gate_act)
        hidden = (gate_act * sigmoid_gate * up_act).astype(jnp.bfloat16)
        down_grad = jnp.dot(hidden.T, rows_cot, preferred_element_type=jnp.float32)
        d_hidden = jnp.dot(rows_cot, down_mat.T, preferred_element_type=jnp.float32)
        d_gate = (d_hidden * up_act * sigmoid_gate * (1.0 + gate_act * (1.0 - sigmoid_gate))).astype(jnp.bfloat16)
        d_up = (d_hidden * gate_act * sigmoid_gate).astype(jnp.bfloat16)
        gate_grad = jnp.dot(rows_in.T, d_gate, preferred_element_type=jnp.float32)
        up_grad = jnp.dot(rows_in.T, d_up, preferred_element_type=jnp.float32)
        count = picked.shape[0]
        gate_groups = d_gate.astype(jnp.float32).reshape(count, groups, HIDDEN_DEV)
        up_groups = d_up.astype(jnp.float32).reshape(count, groups, HIDDEN_DEV)
        wg_groups = gate_mat.astype(jnp.float32).reshape(width, groups, HIDDEN_DEV)
        wu_groups = up_mat.astype(jnp.float32).reshape(width, groups, HIDDEN_DEV)
        shares = jnp.einsum('mqu,dqu->mqd', gate_groups, wg_groups) + jnp.einsum('mqu,dqu->mqd', up_groups, wu_groups)
        shares = lax.optimization_barrier(shares.astype(jnp.bfloat16)).astype(jnp.float32)
        pick_sum = jnp.sum(shares, axis=1)
        total = total.at[owner_tok].add(jnp.where(valid[:, None], pick_sum, jnp.zeros((), jnp.float32)))
        return total, (gate_grad.astype(jnp.bfloat16), up_grad.astype(jnp.bfloat16), down_grad.astype(jnp.bfloat16))

    empty = jnp.zeros(flat_rows.shape, jnp.float32)
    total, grads = lax.scan(per_expert, empty, (table, w_gate, w_up, w_down))
    grad_input = total.astype(jnp.bfloat16).reshape(tokens.shape)
    return grad_input, grads[0][matching], grads[1][matching], grads[2][matching]
```

```python
import jax
import jax.numpy as jnp
from jax import lax
from jax.sharding import PartitionSpec as P


def from_partner(x, axis, distance):
    return lax.ppermute(x, axis, [(i, i ^ 1 << distance) for i in range(lax.axis_size(axis))])


def column_places(route_flat, owner_table, expert_count, cap_col):
    choices_iota = jnp.arange(expert_count, dtype=jnp.int32)
    onehot = (route_flat[:, None] == choices_iota[None, :]).astype(jnp.int32)
    ranking = jnp.sum(jnp.cumsum(onehot, axis=0) * onehot, axis=1) - 1
    target = jnp.sum(onehot * owner_table[None, :], axis=1)
    position = target * cap_col + ranking
    slot_iota = jnp.arange(expert_count * cap_col, dtype=jnp.int32)
    return slot_iota[:, None] == position[None, :]


def contract_rows(left, right):
    return lax.dot_general(
        left, right, (((0,), (0,)), ((), ())), preferred_element_type=jnp.float32
    )


def contract_units(left, right):
    return lax.dot_general(
        left, right, (((1,), (1,)), ((), ())), preferred_element_type=jnp.float32
    )


def shards(tokens, cotangent, w_gate, w_up, w_down, routes, gates, matching):
    rows_here = tokens.shape[2]
    width = tokens.shape[3]
    topk = routes.shape[3]
    expert_count = lax.axis_size("expert")
    group_count = lax.axis_size("dp")
    cap_col = 3 * group_count * rows_here * topk // (2 * expert_count)
    slot_count = expert_count * cap_col
    column_tok = group_count * rows_here
    self_index = lax.axis_index("expert")
    pair_bit = expert_count.bit_length() - 2
    expert_iota = jnp.arange(expert_count, dtype=jnp.int32)
    partner = jnp.sum(jnp.where(expert_iota == self_index, matching, 0))
    flipped = partner != self_index
    weight_gate = w_gate[0]
    weight_up = w_up[0]
    weight_down = w_down[0]
    swapped = from_partner((weight_gate, weight_up, weight_down), "expert", pair_bit)
    weight_gate = jnp.where(flipped, swapped[0], weight_gate)
    weight_up = jnp.where(flipped, swapped[1], weight_up)
    weight_down = jnp.where(flipped, swapped[2], weight_down)
    labels = (
        lax.all_gather(routes, "dp", axis=1, tiled=True),
        lax.all_gather(gates, "dp", axis=1, tiled=True),
    )
    route_col = labels[0].reshape(column_tok * topk)
    gate_col = labels[1].reshape(column_tok, topk).astype(jnp.float32) / 65536.0
    places = column_places(route_col, matching, expert_count, cap_col)
    place_pick = places.astype(jnp.bfloat16)
    place_tok = jnp.any(places.reshape(slot_count, column_tok, topk), axis=2).astype(jnp.bfloat16)
    column = (
        lax.all_gather(tokens, "dp", axis=1, tiled=True),
        lax.all_gather(cotangent, "dp", axis=1, tiled=True),
    )
    col_in = column[0].reshape(column_tok, width)
    col_cot = column[1].reshape(column_tok, width)
    send_in = jnp.dot(place_tok, col_in, preferred_element_type=jnp.float32).astype(jnp.bfloat16)
    dy_pick = (gate_col[:, :, None] * col_cot[:, None, :].astype(jnp.float32)).astype(jnp.bfloat16)
    send_cot = jnp.dot(
        place_pick, dy_pick.reshape(column_tok * topk, width), preferred_element_type=jnp.float32
    ).astype(jnp.bfloat16)
    arrived = (
        lax.all_to_all(
            send_in.reshape(expert_count, cap_col, width),
            "expert",
            split_axis=0,
            concat_axis=0,
            tiled=True,
        ),
        lax.all_to_all(
            send_cot.reshape(expert_count, cap_col, width),
            "expert",
            split_axis=0,
            concat_axis=0,
            tiled=True,
        ),
    )
    routed_rows = arrived[0].reshape(slot_count, width)
    routed_cot = arrived[1].reshape(slot_count, width)
    gate_act = jnp.dot(routed_rows, weight_gate, preferred_element_type=jnp.float32)
    up_act = jnp.dot(routed_rows, weight_up, preferred_element_type=jnp.float32)
    sigmoid_gate = jax.nn.sigmoid(gate_act)
    hidden = (gate_act * sigmoid_gate * up_act).astype(jnp.bfloat16)
    grad_down_here = contract_rows(hidden, routed_cot).astype(jnp.bfloat16)
    d_hidden = contract_units(routed_cot, weight_down)
    d_gate = (d_hidden * up_act * sigmoid_gate * (1.0 + gate_act * (1.0 - sigmoid_gate))).astype(
        jnp.bfloat16
    )
    d_up = (d_hidden * gate_act * sigmoid_gate).astype(jnp.bfloat16)
    grad_gate_here = contract_rows(routed_rows, d_gate).astype(jnp.bfloat16)
    grad_up_here = contract_rows(routed_rows, d_up).astype(jnp.bfloat16)
    partial_terms = contract_units(d_gate, weight_gate) + contract_units(d_up, weight_up)
    parts = partial_terms.astype(jnp.bfloat16).reshape(expert_count, cap_col, width)
    back = lax.all_to_all(parts, "expert", split_axis=0, concat_axis=0, tiled=True)
    col_sum = contract_rows(place_tok, back.reshape(slot_count, width))
    total = lax.psum_scatter(
        col_sum.reshape(group_count, rows_here, width).astype(jnp.bfloat16),
        "dp",
        scatter_dimension=0,
        tiled=True,
    )
    return (
        total.reshape(1, 1, rows_here, width),
        grad_gate_here[None],
        grad_up_here[None],
        grad_down_here[None],
    )


def dense_shards(tokens, cotangent, w_gate, w_up, w_down, routes, gates, matching):
    axes = ("expert", "dp")
    rows_here, width = tokens.shape[2:]
    topk = routes.shape[3]
    units = w_gate.shape[2]
    expert_count = lax.axis_size("expert")
    group_count = lax.axis_size("dp")
    cap_col = 3 * group_count * rows_here * topk // (2 * expert_count)
    slot_count = expert_count * cap_col
    self_index = lax.axis_index("expert")
    pair_bit = expert_count.bit_length() - 2
    expert_iota = jnp.arange(expert_count, dtype=jnp.int32)
    partner = jnp.sum(jnp.where(expert_iota == self_index, matching, 0))
    flipped = partner != self_index
    labels = jnp.concatenate([routes[0, 0], gates[0, 0]], axis=1)
    labels = lax.all_gather(labels, axes, axis=0, tiled=True)
    rows = lax.all_gather(tokens[0, 0], axes, axis=0, tiled=True)
    cots = lax.all_gather(cotangent[0, 0], axes, axis=0, tiled=True)
    route, gate = labels[:, :topk], labels[:, topk:]
    count = route.shape[0]

    def picks(expert):
        hit = jnp.any(route == expert, axis=1)
        at = jnp.arange(count, dtype=jnp.int32)
        ranking = jnp.sum((at[None, :] < at[:, None]) & hit[None, :], axis=1, dtype=jnp.int32)
        slots = jnp.arange(slot_count, dtype=jnp.int32)
        return ((ranking[None, :] == slots[:, None]) & hit[None, :]).astype(jnp.bfloat16)

    weight = jnp.sum(jnp.where(route == self_index, gate, 0), axis=1).astype(jnp.float32) / 65536.0
    weight = weight[:, None]
    gate_act = jnp.dot(rows, w_gate[0], preferred_element_type=jnp.float32)
    up_act = jnp.dot(rows, w_up[0], preferred_element_type=jnp.float32)
    d_hidden = contract_units(cots, w_down[0]) * weight
    sigmoid_gate = jax.nn.sigmoid(gate_act)
    hidden = (gate_act * sigmoid_gate * up_act * weight).astype(jnp.bfloat16)
    d_gate = (d_hidden * up_act * sigmoid_gate * (1.0 + gate_act * (1.0 - sigmoid_gate))).astype(
        jnp.bfloat16
    )
    d_up = (d_hidden * gate_act * sigmoid_gate).astype(jnp.bfloat16)
    factors = jnp.concatenate([d_gate, d_up, hidden], axis=1)
    packed = jnp.dot(picks(self_index), factors, preferred_element_type=jnp.float32)
    packed = packed.astype(jnp.bfloat16)
    swapped = from_partner(packed, "expert", pair_bit)
    partial = contract_units(d_gate, w_gate[0]) + contract_units(d_up, w_up[0])
    total = lax.psum_scatter(
        partial.astype(jnp.bfloat16).reshape(-1, rows_here, width),
        axes,
        scatter_dimension=0,
        tiled=True,
    )
    chosen = jnp.where(flipped, swapped, packed)
    spread = contract_rows(picks(partner), chosen).astype(jnp.bfloat16)
    grad_gate = contract_rows(rows, spread[:, :units]).astype(jnp.bfloat16)
    grad_up = contract_rows(rows, spread[:, units : 2 * units]).astype(jnp.bfloat16)
    grad_down = contract_rows(spread[:, 2 * units :], cots).astype(jnp.bfloat16)
    return (
        total.reshape(1, 1, rows_here, width),
        grad_gate[None],
        grad_up[None],
        grad_down[None],
    )


DENSE_ROWS = 1024


def step(tokens, *rest):
    rows = lax.axis_size("expert") * lax.axis_size("dp") * tokens.shape[2]
    return (dense_shards if rows <= DENSE_ROWS else shards)(tokens, *rest)


def solution(mesh):
    placed = (
        P("expert", "dp", None, None),
        P("expert", "dp", None, None),
        P("expert", None, "dp"),
        P("expert", None, "dp"),
        P("expert", "dp", None),
        P("expert", "dp", None, None),
        P("expert", "dp", None, None),
        P(),
    )
    return jax.shard_map(
        step,
        mesh=mesh,
        in_specs=placed,
        out_specs=(
            P("expert", "dp", None, None),
            P("expert", None, "dp"),
            P("expert", None, "dp"),
            P("expert", "dp", None),
        ),
        check_vma=False,
    )
```

```python
import jax
import jax.numpy as jnp
import numpy as np
from jax import lax
from jax.experimental import pallas as pl
from jax.experimental.pallas import tpu as pltpu
from jax.sharding import PartitionSpec as P

MESH = pl.DeviceIdType.MESH
LANES = 128
ROW_TILE = 8
CHUNKS = 2


def from_partner(x, axis, distance):
    return lax.ppermute(x, axis, [(i, i ^ 1 << distance) for i in range(lax.axis_size(axis))])


def column_places(route_flat, owner_table, expert_count, cap_col):
    choices_iota = jnp.arange(expert_count, dtype=jnp.int32)
    onehot = (route_flat[:, None] == choices_iota[None, :]).astype(jnp.int32)
    ranking = jnp.sum(jnp.cumsum(onehot, axis=0) * onehot, axis=1) - 1
    target = jnp.sum(onehot * owner_table[None, :], axis=1)
    position = target * cap_col + ranking
    slot_iota = jnp.arange(expert_count * cap_col, dtype=jnp.int32)
    return slot_iota[:, None] == position[None, :]


def contract_rows(left, right):
    return lax.dot_general(
        left, right, (((0,), (0,)), ((), ())), preferred_element_type=jnp.float32
    )


def contract_units(left, right):
    return lax.dot_general(
        left, right, (((1,), (1,)), ((), ())), preferred_element_type=jnp.float32
    )


def shards(tokens, cotangent, w_gate, w_up, w_down, routes, gates, matching):
    rows_here = tokens.shape[2]
    width = tokens.shape[3]
    topk = routes.shape[3]
    expert_count = lax.axis_size("expert")
    group_count = lax.axis_size("dp")
    cap_col = 3 * group_count * rows_here * topk // (2 * expert_count)
    slot_count = expert_count * cap_col
    column_tok = group_count * rows_here
    self_index = lax.axis_index("expert")
    pair_bit = expert_count.bit_length() - 2
    expert_iota = jnp.arange(expert_count, dtype=jnp.int32)
    partner = jnp.sum(jnp.where(expert_iota == self_index, matching, 0))
    flipped = partner != self_index
    weight_gate = w_gate[0]
    weight_up = w_up[0]
    weight_down = w_down[0]
    swapped = from_partner((weight_gate, weight_up, weight_down), "expert", pair_bit)
    weight_gate = jnp.where(flipped, swapped[0], weight_gate)
    weight_up = jnp.where(flipped, swapped[1], weight_up)
    weight_down = jnp.where(flipped, swapped[2], weight_down)
    labels = (
        lax.all_gather(routes, "dp", axis=1, tiled=True),
        lax.all_gather(gates, "dp", axis=1, tiled=True),
    )
    route_col = labels[0].reshape(column_tok * topk)
    gate_col = labels[1].reshape(column_tok, topk).astype(jnp.float32) / 65536.0
    places = column_places(route_col, matching, expert_count, cap_col)
    place_pick = places.astype(jnp.bfloat16)
    place_tok = jnp.any(places.reshape(slot_count, column_tok, topk), axis=2).astype(jnp.bfloat16)
    column = (
        lax.all_gather(tokens, "dp", axis=1, tiled=True),
        lax.all_gather(cotangent, "dp", axis=1, tiled=True),
    )
    col_in = column[0].reshape(column_tok, width)
    col_cot = column[1].reshape(column_tok, width)
    send_in = jnp.dot(place_tok, col_in, preferred_element_type=jnp.float32).astype(jnp.bfloat16)
    dy_pick = (gate_col[:, :, None] * col_cot[:, None, :].astype(jnp.float32)).astype(jnp.bfloat16)
    send_cot = jnp.dot(
        place_pick, dy_pick.reshape(column_tok * topk, width), preferred_element_type=jnp.float32
    ).astype(jnp.bfloat16)
    arrived = (
        lax.all_to_all(
            send_in.reshape(expert_count, cap_col, width),
            "expert",
            split_axis=0,
            concat_axis=0,
            tiled=True,
        ),
        lax.all_to_all(
            send_cot.reshape(expert_count, cap_col, width),
            "expert",
            split_axis=0,
            concat_axis=0,
            tiled=True,
        ),
    )
    routed_rows = arrived[0].reshape(slot_count, width)
    routed_cot = arrived[1].reshape(slot_count, width)
    gate_act = jnp.dot(routed_rows, weight_gate, preferred_element_type=jnp.float32)
    up_act = jnp.dot(routed_rows, weight_up, preferred_element_type=jnp.float32)
    sigmoid_gate = jax.nn.sigmoid(gate_act)
    hidden = (gate_act * sigmoid_gate * up_act).astype(jnp.bfloat16)
    grad_down_here = contract_rows(hidden, routed_cot).astype(jnp.bfloat16)
    d_hidden = contract_units(routed_cot, weight_down)
    d_gate = (d_hidden * up_act * sigmoid_gate * (1.0 + gate_act * (1.0 - sigmoid_gate))).astype(
        jnp.bfloat16
    )
    d_up = (d_hidden * gate_act * sigmoid_gate).astype(jnp.bfloat16)
    grad_gate_here = contract_rows(routed_rows, d_gate).astype(jnp.bfloat16)
    grad_up_here = contract_rows(routed_rows, d_up).astype(jnp.bfloat16)
    partial_terms = contract_units(d_gate, weight_gate) + contract_units(d_up, weight_up)
    parts = partial_terms.astype(jnp.bfloat16).reshape(expert_count, cap_col, width)
    back = lax.all_to_all(parts, "expert", split_axis=0, concat_axis=0, tiled=True)
    col_sum = contract_rows(place_tok, back.reshape(slot_count, width))
    total = lax.psum_scatter(
        col_sum.reshape(group_count, rows_here, width).astype(jnp.bfloat16),
        "dp",
        scatter_dimension=0,
        tiled=True,
    )
    return (
        total.reshape(1, 1, rows_here, width),
        grad_gate_here[None],
        grad_up_here[None],
        grad_down_here[None],
    )


def flip(index, bit):
    return index + bit - 2 * bit * lax.rem(lax.div(index, bit), 2)


def greet(peers):
    barrier = pltpu.get_barrier_semaphore()
    for peer in peers:
        place = {"expert": peer[0], "dp": peer[1]}
        pl.semaphore_signal(barrier, inc=1, device_id=place, device_id_type=MESH)
    pl.semaphore_wait(barrier, len(peers))


def remote(src, dst, sems, index, peer):
    return pltpu.make_async_remote_copy(
        src_ref=src,
        dst_ref=dst,
        send_sem=sems[0].at[index],
        recv_sem=sems[1].at[index],
        device_id={"expert": peer[0], "dp": peer[1]},
        device_id_type=MESH,
    )


def gather_kernel(own_ref, out_ref, local_sem, send_sem, recv_sem):
    me, group = lax.axis_index("expert"), lax.axis_index("dp")
    sems = (send_sem, recv_sem)
    along_x, along_y = (me, flip(group, 1)), (me, flip(group, 2))
    near, far, sibling = (flip(me, 2), group), (flip(me, 4), group), (flip(me, 1), group)
    level = [me, flip(me, 2), flip(me, 4), flip(flip(me, 4), 2)]
    spot = [group, flip(group, 1), flip(group, 2), flip(flip(group, 2), 1)]
    z_at, x_at, y_at, diag_at, sib_at = 0, 4, 8, 12, 20
    copies = {}

    def slab(z, d):
        return out_ref.at[:, level[z], spot[d]]

    def send(index, src, dst, peer):
        copies[index] = remote(src, dst, sems, index, peer)
        copies[index].start()

    def arrived(index):
        copies[index].wait_recv()

    greet([along_x, along_y, near, far, sibling])
    keep = pltpu.make_async_copy(own_ref, slab(0, 0), local_sem)
    keep.start()

    def spread(z):
        src = own_ref if z == 0 else slab(z, 0)
        send(x_at + z, src, slab(z, 0), along_x)
        send(y_at + z, src, slab(z, 0), along_y)
        send(sib_at + 4 * z, src, slab(z, 0), sibling)

    def corners(z):
        for d, at, half, peer in ((1, x_at, 0, along_y), (2, y_at, 1, along_x)):
            arrived(at + z)
            part = out_ref.at[half, level[z], spot[d]]
            send(diag_at + 2 * z + half, part, part, peer)
            send(sib_at + 4 * z + d, slab(z, d), slab(z, d), sibling)

    def finish(z):
        for half in range(2):
            arrived(diag_at + 2 * z + half)
        send(sib_at + 4 * z + 3, slab(z, 3), slab(z, 3), sibling)

    send(z_at + 2, own_ref, slab(0, 0), far)
    send(z_at + 1, own_ref, slab(0, 0), near)
    spread(0)
    corners(0)
    arrived(z_at + 1)
    spread(1)
    arrived(z_at + 2)
    send(z_at + 3, slab(2, 0), slab(2, 0), near)
    spread(2)
    finish(0)
    corners(1)
    arrived(z_at + 3)
    spread(3)
    corners(2)
    finish(1)
    corners(3)
    finish(2)
    finish(3)
    for z in range(4):
        for d in range(4):
            arrived(sib_at + 4 * z + d)
    for copy in copies.values():
        copy.wait_send()
    keep.wait()


def gather_all(own):
    halves, rows, columns = own.shape
    experts, groups = lax.axis_size("expert"), lax.axis_size("dp")
    return pl.pallas_call(
        gather_kernel,
        out_shape=jax.ShapeDtypeStruct((halves, experts, groups, rows, columns), own.dtype),
        in_specs=[pl.BlockSpec(memory_space=pl.ANY)],
        out_specs=pl.BlockSpec(memory_space=pl.ANY),
        scratch_shapes=[
            pltpu.SemaphoreType.DMA,
            pltpu.SemaphoreType.DMA((36,)),
            pltpu.SemaphoreType.DMA((36,)),
        ],
        compiler_params=pltpu.CompilerParams(collective_id=0, has_side_effects=True),
    )(own)


def return_kernel(
    parts_ref, packed_ref, widen_ref, place_ref, out_ref, swapped_ref,
    first, second, second_in, third, third_in, send_sem, recv_sem,
):
    me, group = lax.axis_index("expert"), lax.axis_index("dp")
    experts = second.shape[1]
    sems = (send_sem, recv_sem)
    mates = [group, flip(group, 1), flip(group, 2), flip(flip(group, 2), 1)]
    others = [lax.rem(me + m, experts) for m in range(experts)]
    step = 6 + experts
    copies = {}

    def send(index, src, dst, peer):
        copies[index] = remote(src, dst, sems, index, peer)
        copies[index].start()

    greet([(me, mates[r]) for r in (1, 2, 3)] + [(others[m], group) for m in range(1, experts)])
    send(CHUNKS * step, packed_ref, swapped_ref, (flip(me, experts // 2), group))
    for c in range(CHUNKS):
        for r in (3, 1, 2):
            send(c * step + r, parts_ref.at[mates[r] * CHUNKS + c], first.at[c, r], (me, mates[r]))
    for c in range(CHUNKS):
        total = parts_ref[group * CHUNKS + c].astype(jnp.float32)
        for r in (1, 2, 3):
            copies[c * step + r].wait_recv()
            total = total + first[c, r].astype(jnp.float32)
        total = total.astype(jnp.bfloat16)
        for i in range(experts):
            block = jnp.dot(widen_ref[i], total, preferred_element_type=jnp.float32)
            second[c, i] = block.astype(jnp.bfloat16)
        for m in (4, 5, 3, 6, 2, 7, 1):
            send(c * step + 3 + m, second.at[c, others[m]], second_in.at[c, me], (others[m], group))
        second_in[c, me] = second[c, me]
    for c in range(CHUNKS):
        for m in range(1, experts):
            copies[c * step + 3 + m].wait_recv()
        total = jnp.zeros((place_ref.shape[1], second.shape[3]), jnp.float32)
        for i in range(experts):
            total = total + jnp.dot(
                place_ref[i], second_in[c, i], preferred_element_type=jnp.float32
            )
        total = total.astype(jnp.bfloat16)
        rows = third.shape[2]
        for r in range(4):
            third[c, r] = total[r * rows : (r + 1) * rows]
        for r in (3, 1, 2):
            send(c * step + 2 + experts + r, third.at[c, mates[r]], third_in.at[c, group], (me, mates[r]))
        third_in[c, group] = third[c, group]
    for c in range(CHUNKS):
        for r in (1, 2, 3):
            copies[c * step + 2 + experts + r].wait_recv()
        columns = third.shape[3]
        for r in range(4):
            at = (r * CHUNKS + c) * columns
            out_ref[:, at : at + columns] = third_in[c, r]
    copies[CHUNKS * step].wait_recv()
    for copy in copies.values():
        copy.wait_send()


def return_all(parts, packed, widen, place, rows_out):
    pieces, slots, columns = parts.shape
    experts, wide = widen.shape[:2]
    groups = pieces // CHUNKS
    vmem = pl.BlockSpec(memory_space=pltpu.VMEM)
    count = CHUNKS * (6 + experts) + 1
    return pl.pallas_call(
        return_kernel,
        out_shape=(
            jax.ShapeDtypeStruct((rows_out, pieces * columns), jnp.bfloat16),
            jax.ShapeDtypeStruct(packed.shape, packed.dtype),
        ),
        in_specs=[vmem] * 4,
        out_specs=(vmem, vmem),
        scratch_shapes=[
            pltpu.VMEM((CHUNKS, 4, slots, columns), jnp.bfloat16),
            pltpu.VMEM((CHUNKS, experts, wide, columns), jnp.bfloat16),
            pltpu.VMEM((CHUNKS, experts, wide, columns), jnp.bfloat16),
            pltpu.VMEM((CHUNKS, groups, rows_out, columns), jnp.bfloat16),
            pltpu.VMEM((CHUNKS, groups, rows_out, columns), jnp.bfloat16),
            pltpu.SemaphoreType.DMA((count,)),
            pltpu.SemaphoreType.DMA((count,)),
        ],
        compiler_params=pltpu.CompilerParams(
            collective_id=1, has_side_effects=True, vmem_limit_bytes=48 * 2**20
        ),
    )(parts, packed, widen, place)


def small_shards(tokens, cotangent, w_gate, w_up, w_down, routes, gates, matching):
    rows_here, width = tokens.shape[2:]
    topk = routes.shape[3]
    units = w_gate.shape[2]
    half = width // 2
    expert_count = lax.axis_size("expert")
    group_count = lax.axis_size("dp")
    column_tok = group_count * rows_here
    cap_col = 3 * group_count * rows_here * topk // (2 * expert_count)
    slot_count = expert_count * cap_col
    self_index = lax.axis_index("expert")
    expert_iota = jnp.arange(expert_count, dtype=jnp.int32)
    partner = jnp.sum(jnp.where(expert_iota == self_index, matching, 0))
    flipped = partner != self_index
    gate_here = gates[0, 0]
    labels = jnp.concatenate([routes[0, 0], gate_here // 256, gate_here % 256], axis=1)
    labels = jnp.pad(labels, ((0, rows_here), (0, LANES - 3 * topk))).astype(jnp.bfloat16)
    body = jnp.concatenate([tokens[0, 0], cotangent[0, 0]], axis=0)
    own = jnp.stack(
        [
            jnp.concatenate([body[:, :half], labels], axis=1),
            jnp.concatenate([body[:, half:], labels], axis=1),
        ]
    )
    everything = gather_all(own)
    labels = everything[0, :, :, :rows_here, half : half + 3 * topk].astype(jnp.int32)
    labels = labels.reshape(expert_count, column_tok, 3, topk)
    route = labels[:, :, 0]
    gate = labels[:, :, 1] * 256 + labels[:, :, 2]
    rows_all = everything.reshape(2, expert_count * group_count * 2 * rows_here, half + LANES)

    def ranked(expert):
        hit = jnp.any(route == expert, axis=2)
        at = jnp.arange(column_tok, dtype=jnp.int32)
        before = (at[None, :] < at[:, None])[None] & hit[:, None, :]
        ranking = jnp.sum(before, axis=2, dtype=jnp.int32)
        slot = expert_iota[:, None] * cap_col + ranking
        return jnp.where(hit, slot, -1).reshape(expert_count, group_count, rows_here)

    def picked(expert):
        slot = ranked(expert)
        none = jnp.full_like(slot, -1)
        from_tok = jnp.concatenate([slot, none], axis=2).reshape(-1)
        from_cot = jnp.concatenate([none, slot], axis=2).reshape(-1)
        iota = jnp.arange(slot_count, dtype=jnp.int32)[:, None]
        pick = jnp.concatenate([from_tok[None] == iota, from_cot[None] == iota], axis=0)
        pick = pick.astype(jnp.bfloat16)
        return [
            jnp.dot(pick, rows_all[i], preferred_element_type=jnp.float32)[:, :half].astype(
                jnp.bfloat16
            )
            for i in range(2)
        ]

    weight = jnp.sum(jnp.where(route == self_index, gate, 0), axis=2).reshape(-1)
    own_slot = ranked(self_index).reshape(-1)
    slot_iota = jnp.arange(slot_count, dtype=jnp.int32)[:, None]
    weight = jnp.sum(jnp.where(own_slot[None] == slot_iota, weight[None], 0), axis=1)
    weight = (weight.astype(jnp.float32) / 65536.0)[:, None]
    mine = picked(self_index)
    rows_in = jnp.concatenate([block[:slot_count] for block in mine], axis=1)
    rows_cot = jnp.concatenate([block[slot_count:] for block in mine], axis=1)
    rows_cot = (rows_cot.astype(jnp.float32) * weight).astype(jnp.bfloat16)
    gate_act = jnp.dot(rows_in, w_gate[0], preferred_element_type=jnp.float32)
    up_act = jnp.dot(rows_in, w_up[0], preferred_element_type=jnp.float32)
    d_hidden = contract_units(rows_cot, w_down[0])
    sigmoid_gate = jax.nn.sigmoid(gate_act)
    hidden = (gate_act * sigmoid_gate * up_act * weight).astype(jnp.bfloat16)
    d_gate = (d_hidden * up_act * sigmoid_gate * (1.0 + gate_act * (1.0 - sigmoid_gate))).astype(
        jnp.bfloat16
    )
    d_up = (d_hidden * gate_act * sigmoid_gate).astype(jnp.bfloat16)
    packed = jnp.concatenate([d_gate, d_up, hidden], axis=1)
    pieces = group_count * CHUNKS
    partial = contract_units(d_gate, w_gate[0]) + contract_units(d_up, w_up[0])
    parts = partial.astype(jnp.bfloat16).reshape(slot_count, pieces, width // pieces)
    parts = parts.transpose(1, 0, 2)
    wide = -(-cap_col // ROW_TILE) * ROW_TILE
    widen = np.zeros((expert_count, wide, slot_count), np.float32)
    for i in range(expert_count):
        widen[i, np.arange(cap_col), i * cap_col + np.arange(cap_col)] = 1.0
    column_route = jnp.sum(
        jnp.where(expert_iota[:, None, None] == self_index, route, 0), axis=0
    )
    hits = jnp.any(column_route[None] == expert_iota[:, None, None], axis=2)
    at = jnp.arange(column_tok, dtype=jnp.int32)
    ranking = jnp.sum(
        (at[None, :] < at[:, None])[None] & hits[:, None, :], axis=2, dtype=jnp.int32
    )
    place = (ranking[:, :, None] == jnp.arange(wide)[None, None]) & hits[:, :, None]
    rows_out = -(-rows_here // 16) * 16
    place = place.reshape(expert_count, group_count, rows_here, wide)
    place = jnp.pad(place, ((0, 0), (0, 0), (0, rows_out - rows_here), (0, 0)))
    place = place.reshape(expert_count, group_count * rows_out, wide).astype(jnp.bfloat16)
    total, swapped = return_all(
        parts, packed, jnp.asarray(widen, jnp.bfloat16), place, rows_out
    )
    chosen = jnp.where(flipped, swapped, packed)
    theirs = picked(partner)
    their_rows = jnp.concatenate([block[:slot_count] for block in theirs], axis=1)
    their_cot = jnp.concatenate([block[slot_count:] for block in theirs], axis=1)
    grad_gate = contract_rows(their_rows, chosen[:, :units]).astype(jnp.bfloat16)
    grad_up = contract_rows(their_rows, chosen[:, units : 2 * units]).astype(jnp.bfloat16)
    grad_down = contract_rows(chosen[:, 2 * units :], their_cot).astype(jnp.bfloat16)
    return (
        total[:rows_here].reshape(1, 1, rows_here, width),
        grad_gate[None],
        grad_up[None],
        grad_down[None],
    )


def step(tokens, *rest):
    small = lax.axis_size("expert") == 8 and lax.axis_size("dp") == 4
    return (small_shards if small else shards)(tokens, *rest)


def solution(mesh):
    placed = (
        P("expert", "dp", None, None),
        P("expert", "dp", None, None),
        P("expert", None, "dp"),
        P("expert", None, "dp"),
        P("expert", "dp", None),
        P("expert", "dp", None, None),
        P("expert", "dp", None, None),
        P(),
    )
    return jax.shard_map(
        step,
        mesh=mesh,
        in_specs=placed,
        out_specs=(
            P("expert", "dp", None, None),
            P("expert", None, "dp"),
            P("expert", None, "dp"),
            P("expert", "dp", None),
        ),
        check_vma=False,
    )
```

```python
import jax
import jax.numpy as jnp
import numpy as np
from jax import lax
from jax.experimental import pallas as pl
from jax.experimental.pallas import tpu as pltpu
from jax.sharding import PartitionSpec as P

MESH = pl.DeviceIdType.MESH
LANES = 128
ROW_TILE = 8
CHUNKS = 7
LAG = 2


def from_partner(x, axis, distance):
    return lax.ppermute(x, axis, [(i, i ^ 1 << distance) for i in range(lax.axis_size(axis))])


def column_places(route_flat, owner_table, expert_count, cap_col):
    choices_iota = jnp.arange(expert_count, dtype=jnp.int32)
    onehot = (route_flat[:, None] == choices_iota[None, :]).astype(jnp.int32)
    ranking = jnp.sum(jnp.cumsum(onehot, axis=0) * onehot, axis=1) - 1
    target = jnp.sum(onehot * owner_table[None, :], axis=1)
    position = target * cap_col + ranking
    slot_iota = jnp.arange(expert_count * cap_col, dtype=jnp.int32)
    return slot_iota[:, None] == position[None, :]


def contract_rows(left, right):
    return lax.dot_general(
        left, right, (((0,), (0,)), ((), ())), preferred_element_type=jnp.float32
    )


def contract_units(left, right):
    return lax.dot_general(
        left, right, (((1,), (1,)), ((), ())), preferred_element_type=jnp.float32
    )


def shards(tokens, cotangent, w_gate, w_up, w_down, routes, gates, matching):
    rows_here = tokens.shape[2]
    width = tokens.shape[3]
    topk = routes.shape[3]
    expert_count = lax.axis_size("expert")
    group_count = lax.axis_size("dp")
    cap_col = 3 * group_count * rows_here * topk // (2 * expert_count)
    slot_count = expert_count * cap_col
    column_tok = group_count * rows_here
    self_index = lax.axis_index("expert")
    pair_bit = expert_count.bit_length() - 2
    expert_iota = jnp.arange(expert_count, dtype=jnp.int32)
    partner = jnp.sum(jnp.where(expert_iota == self_index, matching, 0))
    flipped = partner != self_index
    weight_gate = w_gate[0]
    weight_up = w_up[0]
    weight_down = w_down[0]
    swapped = from_partner((weight_gate, weight_up, weight_down), "expert", pair_bit)
    weight_gate = jnp.where(flipped, swapped[0], weight_gate)
    weight_up = jnp.where(flipped, swapped[1], weight_up)
    weight_down = jnp.where(flipped, swapped[2], weight_down)
    labels = (
        lax.all_gather(routes, "dp", axis=1, tiled=True),
        lax.all_gather(gates, "dp", axis=1, tiled=True),
    )
    route_col = labels[0].reshape(column_tok * topk)
    gate_col = labels[1].reshape(column_tok, topk).astype(jnp.float32) / 65536.0
    places = column_places(route_col, matching, expert_count, cap_col)
    place_pick = places.astype(jnp.bfloat16)
    place_tok = jnp.any(places.reshape(slot_count, column_tok, topk), axis=2).astype(jnp.bfloat16)
    column = (
        lax.all_gather(tokens, "dp", axis=1, tiled=True),
        lax.all_gather(cotangent, "dp", axis=1, tiled=True),
    )
    col_in = column[0].reshape(column_tok, width)
    col_cot = column[1].reshape(column_tok, width)
    send_in = jnp.dot(place_tok, col_in, preferred_element_type=jnp.float32).astype(jnp.bfloat16)
    dy_pick = (gate_col[:, :, None] * col_cot[:, None, :].astype(jnp.float32)).astype(jnp.bfloat16)
    send_cot = jnp.dot(
        place_pick, dy_pick.reshape(column_tok * topk, width), preferred_element_type=jnp.float32
    ).astype(jnp.bfloat16)
    arrived = (
        lax.all_to_all(
            send_in.reshape(expert_count, cap_col, width),
            "expert",
            split_axis=0,
            concat_axis=0,
            tiled=True,
        ),
        lax.all_to_all(
            send_cot.reshape(expert_count, cap_col, width),
            "expert",
            split_axis=0,
            concat_axis=0,
            tiled=True,
        ),
    )
    routed_rows = arrived[0].reshape(slot_count, width)
    routed_cot = arrived[1].reshape(slot_count, width)
    gate_act = jnp.dot(routed_rows, weight_gate, preferred_element_type=jnp.float32)
    up_act = jnp.dot(routed_rows, weight_up, preferred_element_type=jnp.float32)
    sigmoid_gate = jax.nn.sigmoid(gate_act)
    hidden = (gate_act * sigmoid_gate * up_act).astype(jnp.bfloat16)
    grad_down_here = contract_rows(hidden, routed_cot).astype(jnp.bfloat16)
    d_hidden = contract_units(routed_cot, weight_down)
    d_gate = (d_hidden * up_act * sigmoid_gate * (1.0 + gate_act * (1.0 - sigmoid_gate))).astype(
        jnp.bfloat16
    )
    d_up = (d_hidden * gate_act * sigmoid_gate).astype(jnp.bfloat16)
    grad_gate_here = contract_rows(routed_rows, d_gate).astype(jnp.bfloat16)
    grad_up_here = contract_rows(routed_rows, d_up).astype(jnp.bfloat16)
    partial_terms = contract_units(d_gate, weight_gate) + contract_units(d_up, weight_up)
    parts = partial_terms.astype(jnp.bfloat16).reshape(expert_count, cap_col, width)
    back = lax.all_to_all(parts, "expert", split_axis=0, concat_axis=0, tiled=True)
    col_sum = contract_rows(place_tok, back.reshape(slot_count, width))
    total = lax.psum_scatter(
        col_sum.reshape(group_count, rows_here, width).astype(jnp.bfloat16),
        "dp",
        scatter_dimension=0,
        tiled=True,
    )
    return (
        total.reshape(1, 1, rows_here, width),
        grad_gate_here[None],
        grad_up_here[None],
        grad_down_here[None],
    )


def flip(index, bit):
    return index + bit - 2 * bit * lax.rem(lax.div(index, bit), 2)


def greet(peers):
    barrier = pltpu.get_barrier_semaphore()
    for peer in peers:
        place = {"expert": peer[0], "dp": peer[1]}
        pl.semaphore_signal(barrier, inc=1, device_id=place, device_id_type=MESH)
    pl.semaphore_wait(barrier, len(peers))


def remote(src, dst, sems, index, peer):
    return pltpu.make_async_remote_copy(
        src_ref=src,
        dst_ref=dst,
        send_sem=sems[0].at[index],
        recv_sem=sems[1].at[index],
        device_id={"expert": peer[0], "dp": peer[1]},
        device_id_type=MESH,
    )


def gather_kernel(
    tok_ref, cot_ref, route_ref, gate_ref, out_ref, own_ref, local_sem, send_sem, recv_sem
):
    me, group = lax.axis_index("expert"), lax.axis_index("dp")
    sems = (send_sem, recv_sem)
    along_x, along_y = (me, flip(group, 1)), (me, flip(group, 2))
    near, far, sibling = (flip(me, 2), group), (flip(me, 4), group), (flip(me, 1), group)
    level = [me, flip(me, 2), flip(me, 4), flip(flip(me, 4), 2)]
    spot = [group, flip(group, 1), flip(group, 2), flip(flip(group, 2), 1)]
    z_at, x_at, y_at, diag_at, sib_at = 0, 4, 8, 12, 20
    copies = {}
    rows, width = tok_ref.shape
    columns = out_ref.shape[3]
    middle = width // 2
    topk = route_ref.shape[1]
    lane = lax.broadcasted_iota(jnp.int32, (rows, columns - width), 1)
    labels = jnp.zeros_like(lane)
    for k in range(topk):
        gate = gate_ref[:, k : k + 1]
        labels = jnp.where(lane == k, route_ref[:, k : k + 1], labels)
        labels = jnp.where(lane == topk + k, lax.shift_right_logical(gate, 8), labels)
        labels = jnp.where(lane == 2 * topk + k, gate & 255, labels)
    labels = labels.astype(jnp.float32).astype(jnp.bfloat16)
    own_ref[:rows, :width] = tok_ref[...]
    own_ref[rows:, :width] = cot_ref[...]
    own_ref[:rows, width:] = labels
    own_ref[rows:, width:] = jnp.zeros_like(labels)

    def slab(z, d):
        return out_ref.at[level[z], spot[d]]

    def send(index, src, dst, peer):
        copies[index] = remote(src, dst, sems, index, peer)
        copies[index].start()

    def arrived(index):
        copies[index].wait_recv()

    greet([along_x, along_y, near, far, sibling])
    keep = pltpu.make_async_copy(own_ref, slab(0, 0), local_sem)
    keep.start()

    def spread(z):
        src = own_ref if z == 0 else slab(z, 0)
        send(x_at + z, src, slab(z, 0), along_x)
        send(y_at + z, src, slab(z, 0), along_y)
        send(sib_at + 4 * z, src, slab(z, 0), sibling)

    def corners(z):
        for d, at, half, peer in ((1, x_at, 0, along_y), (2, y_at, 1, along_x)):
            arrived(at + z)
            part = slab(z, d).at[:, pl.ds(half * middle, columns - middle if half else middle)]
            send(diag_at + 2 * z + half, part, part, peer)
            send(sib_at + 4 * z + d, slab(z, d), slab(z, d), sibling)

    def finish(z):
        for half in range(2):
            arrived(diag_at + 2 * z + half)
        send(sib_at + 4 * z + 3, slab(z, 3), slab(z, 3), sibling)

    send(z_at + 2, own_ref, slab(0, 0), far)
    send(z_at + 1, own_ref, slab(0, 0), near)
    spread(0)
    corners(0)
    arrived(z_at + 1)
    spread(1)
    arrived(z_at + 2)
    send(z_at + 3, slab(2, 0), slab(2, 0), near)
    spread(2)
    finish(0)
    corners(1)
    arrived(z_at + 3)
    spread(3)
    corners(2)
    finish(1)
    corners(3)
    finish(2)
    finish(3)
    for z in range(4):
        for d in range(4):
            arrived(sib_at + 4 * z + d)
    for copy in copies.values():
        copy.wait_send()
    keep.wait()


def gather_all(tokens, cotangent, routes, gates):
    rows, width = tokens.shape
    columns = width + LANES
    experts, groups = lax.axis_size("expert"), lax.axis_size("dp")
    return pl.pallas_call(
        gather_kernel,
        out_shape=jax.ShapeDtypeStruct((experts, groups, 2 * rows, columns), tokens.dtype),
        in_specs=[pl.BlockSpec(memory_space=pltpu.VMEM)] * 4,
        out_specs=pl.BlockSpec(memory_space=pl.ANY),
        scratch_shapes=[
            pltpu.VMEM((2 * rows, columns), tokens.dtype),
            pltpu.SemaphoreType.DMA,
            pltpu.SemaphoreType.DMA((36,)),
            pltpu.SemaphoreType.DMA((36,)),
        ],
        compiler_params=pltpu.CompilerParams(collective_id=0, has_side_effects=True),
    )(tokens, cotangent, routes, gates)


def return_kernel(
    parts_ref, packed_ref, widen_ref, place_ref, out_ref, swapped_ref,
    first, second, second_in, third, third_in, send_sem, recv_sem,
):
    me, group = lax.axis_index("expert"), lax.axis_index("dp")
    experts = second.shape[1]
    sems = (send_sem, recv_sem)
    mates = [group, flip(group, 1), flip(group, 2), flip(flip(group, 2), 1)]
    others = [lax.rem(me + m, experts) for m in range(experts)]
    step = 6 + experts
    copies = {}

    def send(index, src, dst, peer):
        copies[index] = remote(src, dst, sems, index, peer)
        copies[index].start()

    greet([(me, mates[r]) for r in (1, 2, 3)] + [(others[m], group) for m in range(1, experts)])
    send(CHUNKS * step, packed_ref, swapped_ref, (flip(me, experts // 2), group))
    for c in range(CHUNKS):
        for r in (3, 1, 2):
            send(c * step + r, parts_ref.at[mates[r] * CHUNKS + c], first.at[c, r], (me, mates[r]))

    def back(c):
        total = parts_ref[group * CHUNKS + c].astype(jnp.float32)
        for r in (1, 2, 3):
            copies[c * step + r].wait_recv()
            total = total + first[c, r].astype(jnp.float32)
        total = total.astype(jnp.bfloat16)
        for i in range(experts):
            block = jnp.dot(widen_ref[i], total, preferred_element_type=jnp.float32)
            second[c, i] = block.astype(jnp.bfloat16)
        for m in (4, 5, 3, 6, 2, 7, 1):
            send(c * step + 3 + m, second.at[c, others[m]], second_in.at[c, me], (others[m], group))
        second_in[c, me] = second[c, me]

    def join(c):
        for m in range(1, experts):
            copies[c * step + 3 + m].wait_recv()
        total = jnp.zeros((place_ref.shape[1], second.shape[3]), jnp.float32)
        for i in range(experts):
            total = total + jnp.dot(
                place_ref[i], second_in[c, i], preferred_element_type=jnp.float32
            )
        total = total.astype(jnp.bfloat16)
        rows = third.shape[2]
        for r in range(4):
            third[c, r] = total[r * rows : (r + 1) * rows]
        for r in (3, 1, 2):
            send(c * step + 2 + experts + r, third.at[c, mates[r]], third_in.at[c, group], (me, mates[r]))
        third_in[c, group] = third[c, group]

    for c in range(CHUNKS + LAG):
        if c < CHUNKS:
            back(c)
        if c >= LAG:
            join(c - LAG)
    for c in range(CHUNKS):
        for r in (1, 2, 3):
            copies[c * step + 2 + experts + r].wait_recv()
        columns = third.shape[3]
        for r in range(4):
            at = (r * CHUNKS + c) * columns
            out_ref[:, at : at + columns] = third_in[c, r]
    copies[CHUNKS * step].wait_recv()
    for copy in copies.values():
        copy.wait_send()


def return_all(parts, packed, widen, place, rows_out):
    pieces, slots, columns = parts.shape
    experts, wide = widen.shape[:2]
    groups = pieces // CHUNKS
    vmem = pl.BlockSpec(memory_space=pltpu.VMEM)
    count = CHUNKS * (6 + experts) + 1
    return pl.pallas_call(
        return_kernel,
        out_shape=(
            jax.ShapeDtypeStruct((rows_out, pieces * columns), jnp.bfloat16),
            jax.ShapeDtypeStruct(packed.shape, packed.dtype),
        ),
        in_specs=[vmem] * 4,
        out_specs=(vmem, vmem),
        scratch_shapes=[
            pltpu.VMEM((CHUNKS, 4, slots, columns), jnp.bfloat16),
            pltpu.VMEM((CHUNKS, experts, wide, columns), jnp.bfloat16),
            pltpu.VMEM((CHUNKS, experts, wide, columns), jnp.bfloat16),
            pltpu.VMEM((CHUNKS, groups, rows_out, columns), jnp.bfloat16),
            pltpu.VMEM((CHUNKS, groups, rows_out, columns), jnp.bfloat16),
            pltpu.SemaphoreType.DMA((count,)),
            pltpu.SemaphoreType.DMA((count,)),
        ],
        compiler_params=pltpu.CompilerParams(
            collective_id=1, has_side_effects=True, vmem_limit_bytes=48 * 2**20
        ),
    )(parts, packed, widen, place)


def small_shards(tokens, cotangent, w_gate, w_up, w_down, routes, gates, matching):
    rows_here, width = tokens.shape[2:]
    topk = routes.shape[3]
    units = w_gate.shape[2]
    expert_count = lax.axis_size("expert")
    group_count = lax.axis_size("dp")
    column_tok = group_count * rows_here
    cap_col = 3 * group_count * rows_here * topk // (2 * expert_count)
    slot_count = expert_count * cap_col
    self_index = lax.axis_index("expert")
    expert_iota = jnp.arange(expert_count, dtype=jnp.int32)
    partner = jnp.sum(jnp.where(expert_iota == self_index, matching, 0))
    flipped = partner != self_index
    everything = gather_all(tokens[0, 0], cotangent[0, 0], routes[0, 0], gates[0, 0])
    labels = everything[:, :, :rows_here, width : width + 3 * topk].astype(jnp.int32)
    labels = labels.reshape(expert_count, column_tok, 3, topk)
    route = labels[:, :, 0]
    gate = labels[:, :, 1] * 256 + labels[:, :, 2]
    rows_all = everything.reshape(expert_count * group_count * 2 * rows_here, width + LANES)

    def ranked(expert):
        hit = jnp.any(route == expert, axis=2)
        at = jnp.arange(column_tok, dtype=jnp.int32)
        before = (at[None, :] < at[:, None])[None] & hit[:, None, :]
        ranking = jnp.sum(before, axis=2, dtype=jnp.int32)
        slot = expert_iota[:, None] * cap_col + ranking
        return jnp.where(hit, slot, -1).reshape(expert_count, group_count, rows_here)

    def picked(expert):
        slot = ranked(expert)
        none = jnp.full_like(slot, -1)
        from_tok = jnp.concatenate([slot, none], axis=2).reshape(-1)
        from_cot = jnp.concatenate([none, slot], axis=2).reshape(-1)
        iota = jnp.arange(slot_count, dtype=jnp.int32)[:, None]
        pick = jnp.concatenate([from_tok[None] == iota, from_cot[None] == iota], axis=0)
        pick = pick.astype(jnp.bfloat16)
        both = jnp.dot(pick, rows_all, preferred_element_type=jnp.float32).astype(jnp.bfloat16)
        return both[:slot_count, :width], both[slot_count:, :width]

    weight = jnp.sum(jnp.where(route == self_index, gate, 0), axis=2).reshape(-1)
    own_slot = ranked(self_index).reshape(-1)
    slot_iota = jnp.arange(slot_count, dtype=jnp.int32)[:, None]
    weight = jnp.sum(jnp.where(own_slot[None] == slot_iota, weight[None], 0), axis=1)
    weight = (weight.astype(jnp.float32) / 65536.0)[:, None]
    rows_in, rows_cot = picked(self_index)
    rows_cot = (rows_cot.astype(jnp.float32) * weight).astype(jnp.bfloat16)
    gate_act = jnp.dot(rows_in, w_gate[0], preferred_element_type=jnp.float32)
    up_act = jnp.dot(rows_in, w_up[0], preferred_element_type=jnp.float32)
    d_hidden = contract_units(rows_cot, w_down[0])
    sigmoid_gate = jax.nn.sigmoid(gate_act)
    hidden = (gate_act * sigmoid_gate * up_act * weight).astype(jnp.bfloat16)
    d_gate = (d_hidden * up_act * sigmoid_gate * (1.0 + gate_act * (1.0 - sigmoid_gate))).astype(
        jnp.bfloat16
    )
    d_up = (d_hidden * gate_act * sigmoid_gate).astype(jnp.bfloat16)
    packed = jnp.concatenate([d_gate, d_up, hidden], axis=1)
    pieces = group_count * CHUNKS
    partial = contract_units(d_gate, w_gate[0]) + contract_units(d_up, w_up[0])
    parts = partial.astype(jnp.bfloat16).reshape(slot_count, pieces, width // pieces)
    parts = parts.transpose(1, 0, 2)
    wide = -(-cap_col // ROW_TILE) * ROW_TILE
    widen = np.zeros((expert_count, wide, slot_count), np.float32)
    for i in range(expert_count):
        widen[i, np.arange(cap_col), i * cap_col + np.arange(cap_col)] = 1.0
    column_route = jnp.sum(
        jnp.where(expert_iota[:, None, None] == self_index, route, 0), axis=0
    )
    hits = jnp.any(column_route[None] == expert_iota[:, None, None], axis=2)
    at = jnp.arange(column_tok, dtype=jnp.int32)
    ranking = jnp.sum(
        (at[None, :] < at[:, None])[None] & hits[:, None, :], axis=2, dtype=jnp.int32
    )
    place = (ranking[:, :, None] == jnp.arange(wide)[None, None]) & hits[:, :, None]
    rows_out = -(-rows_here // 16) * 16
    place = place.reshape(expert_count, group_count, rows_here, wide)
    place = jnp.pad(place, ((0, 0), (0, 0), (0, rows_out - rows_here), (0, 0)))
    place = place.reshape(expert_count, group_count * rows_out, wide).astype(jnp.bfloat16)
    total, swapped = return_all(
        parts, packed, jnp.asarray(widen, jnp.bfloat16), place, rows_out
    )
    chosen = jnp.where(flipped, swapped, packed)
    their_rows, their_cot = picked(partner)
    grad_gate = contract_rows(their_rows, chosen[:, :units]).astype(jnp.bfloat16)
    grad_up = contract_rows(their_rows, chosen[:, units : 2 * units]).astype(jnp.bfloat16)
    grad_down = contract_rows(chosen[:, 2 * units :], their_cot).astype(jnp.bfloat16)
    return (
        total[:rows_here].reshape(1, 1, rows_here, width),
        grad_gate[None],
        grad_up[None],
        grad_down[None],
    )


def step(tokens, *rest):
    small = lax.axis_size("expert") == 8 and lax.axis_size("dp") == 4
    return (small_shards if small else shards)(tokens, *rest)


def solution(mesh):
    placed = (
        P("expert", "dp", None, None),
        P("expert", "dp", None, None),
        P("expert", None, "dp"),
        P("expert", None, "dp"),
        P("expert", "dp", None),
        P("expert", "dp", None, None),
        P("expert", "dp", None, None),
        P(),
    )
    return jax.shard_map(
        step,
        mesh=mesh,
        in_specs=placed,
        out_specs=(
            P("expert", "dp", None, None),
            P("expert", None, "dp"),
            P("expert", None, "dp"),
            P("expert", "dp", None),
        ),
        check_vma=False,
    )
```

```python
import jax
import jax.numpy as jnp
import numpy as np
from jax import lax
from jax.experimental import pallas as pl
from jax.experimental.pallas import tpu as pltpu
from jax.sharding import PartitionSpec as P

MESH = pl.DeviceIdType.MESH
LANES = 128
ROW_TILE = 8
CHUNKS = 7
LAG = 2


def from_partner(x, axis, distance):
    return lax.ppermute(x, axis, [(i, i ^ 1 << distance) for i in range(lax.axis_size(axis))])


def column_places(route_flat, owner_table, expert_count, cap_col):
    choices_iota = jnp.arange(expert_count, dtype=jnp.int32)
    onehot = (route_flat[:, None] == choices_iota[None, :]).astype(jnp.int32)
    ranking = jnp.sum(jnp.cumsum(onehot, axis=0) * onehot, axis=1) - 1
    target = jnp.sum(onehot * owner_table[None, :], axis=1)
    position = target * cap_col + ranking
    slot_iota = jnp.arange(expert_count * cap_col, dtype=jnp.int32)
    return slot_iota[:, None] == position[None, :]


def contract_rows(left, right):
    return lax.dot_general(
        left, right, (((0,), (0,)), ((), ())), preferred_element_type=jnp.float32
    )


def contract_units(left, right):
    return lax.dot_general(
        left, right, (((1,), (1,)), ((), ())), preferred_element_type=jnp.float32
    )


def shards(tokens, cotangent, w_gate, w_up, w_down, routes, gates, matching):
    rows_here = tokens.shape[2]
    width = tokens.shape[3]
    topk = routes.shape[3]
    expert_count = lax.axis_size("expert")
    group_count = lax.axis_size("dp")
    cap_col = 3 * group_count * rows_here * topk // (2 * expert_count)
    slot_count = expert_count * cap_col
    column_tok = group_count * rows_here
    self_index = lax.axis_index("expert")
    pair_bit = expert_count.bit_length() - 2
    expert_iota = jnp.arange(expert_count, dtype=jnp.int32)
    partner = jnp.sum(jnp.where(expert_iota == self_index, matching, 0))
    flipped = partner != self_index
    weight_gate = w_gate[0]
    weight_up = w_up[0]
    weight_down = w_down[0]
    swapped = from_partner((weight_gate, weight_up, weight_down), "expert", pair_bit)
    weight_gate = jnp.where(flipped, swapped[0], weight_gate)
    weight_up = jnp.where(flipped, swapped[1], weight_up)
    weight_down = jnp.where(flipped, swapped[2], weight_down)
    labels = (
        lax.all_gather(routes, "dp", axis=1, tiled=True),
        lax.all_gather(gates, "dp", axis=1, tiled=True),
    )
    route_col = labels[0].reshape(column_tok * topk)
    gate_col = labels[1].reshape(column_tok, topk).astype(jnp.float32) / 65536.0
    places = column_places(route_col, matching, expert_count, cap_col)
    place_pick = places.astype(jnp.bfloat16)
    place_tok = jnp.any(places.reshape(slot_count, column_tok, topk), axis=2).astype(jnp.bfloat16)
    column = (
        lax.all_gather(tokens, "dp", axis=1, tiled=True),
        lax.all_gather(cotangent, "dp", axis=1, tiled=True),
    )
    col_in = column[0].reshape(column_tok, width)
    col_cot = column[1].reshape(column_tok, width)
    send_in = jnp.dot(place_tok, col_in, preferred_element_type=jnp.float32).astype(jnp.bfloat16)
    dy_pick = (gate_col[:, :, None] * col_cot[:, None, :].astype(jnp.float32)).astype(jnp.bfloat16)
    send_cot = jnp.dot(
        place_pick, dy_pick.reshape(column_tok * topk, width), preferred_element_type=jnp.float32
    ).astype(jnp.bfloat16)
    arrived = (
        lax.all_to_all(
            send_in.reshape(expert_count, cap_col, width),
            "expert",
            split_axis=0,
            concat_axis=0,
            tiled=True,
        ),
        lax.all_to_all(
            send_cot.reshape(expert_count, cap_col, width),
            "expert",
            split_axis=0,
            concat_axis=0,
            tiled=True,
        ),
    )
    routed_rows = arrived[0].reshape(slot_count, width)
    routed_cot = arrived[1].reshape(slot_count, width)
    gate_act = jnp.dot(routed_rows, weight_gate, preferred_element_type=jnp.float32)
    up_act = jnp.dot(routed_rows, weight_up, preferred_element_type=jnp.float32)
    sigmoid_gate = jax.nn.sigmoid(gate_act)
    hidden = (gate_act * sigmoid_gate * up_act).astype(jnp.bfloat16)
    grad_down_here = contract_rows(hidden, routed_cot).astype(jnp.bfloat16)
    d_hidden = contract_units(routed_cot, weight_down)
    d_gate = (d_hidden * up_act * sigmoid_gate * (1.0 + gate_act * (1.0 - sigmoid_gate))).astype(
        jnp.bfloat16
    )
    d_up = (d_hidden * gate_act * sigmoid_gate).astype(jnp.bfloat16)
    grad_gate_here = contract_rows(routed_rows, d_gate).astype(jnp.bfloat16)
    grad_up_here = contract_rows(routed_rows, d_up).astype(jnp.bfloat16)
    partial_terms = contract_units(d_gate, weight_gate) + contract_units(d_up, weight_up)
    parts = partial_terms.astype(jnp.bfloat16).reshape(expert_count, cap_col, width)
    back = lax.all_to_all(parts, "expert", split_axis=0, concat_axis=0, tiled=True)
    col_sum = contract_rows(place_tok, back.reshape(slot_count, width))
    total = lax.psum_scatter(
        col_sum.reshape(group_count, rows_here, width).astype(jnp.bfloat16),
        "dp",
        scatter_dimension=0,
        tiled=True,
    )
    return (
        total.reshape(1, 1, rows_here, width),
        grad_gate_here[None],
        grad_up_here[None],
        grad_down_here[None],
    )


def flip(index, bit):
    return index + bit - 2 * bit * lax.rem(lax.div(index, bit), 2)


def greet(peers):
    barrier = pltpu.get_barrier_semaphore()
    for peer in peers:
        place = {"expert": peer[0], "dp": peer[1]}
        pl.semaphore_signal(barrier, inc=1, device_id=place, device_id_type=MESH)
    pl.semaphore_wait(barrier, len(peers))


def remote(src, dst, sems, index, peer):
    return pltpu.make_async_remote_copy(
        src_ref=src,
        dst_ref=dst,
        send_sem=sems[0].at[index],
        recv_sem=sems[1].at[index],
        device_id={"expert": peer[0], "dp": peer[1]},
        device_id_type=MESH,
    )


def gather_kernel(
    tok_ref, cot_ref, route_ref, gate_ref, out_ref, own_ref, local_sem, send_sem, recv_sem
):
    me, group = lax.axis_index("expert"), lax.axis_index("dp")
    sems = (send_sem, recv_sem)
    along_x, along_y = (me, flip(group, 1)), (me, flip(group, 2))
    near, far, sibling = (flip(me, 2), group), (flip(me, 4), group), (flip(me, 1), group)
    level = [me, flip(me, 2), flip(me, 4), flip(flip(me, 4), 2)]
    spot = [group, flip(group, 1), flip(group, 2), flip(flip(group, 2), 1)]
    z_at, x_at, y_at, diag_at, sib_at = 0, 4, 8, 12, 20
    copies = {}
    rows, width = tok_ref.shape
    columns = out_ref.shape[3]
    middle = width // 2
    topk = route_ref.shape[1]
    lane = lax.broadcasted_iota(jnp.int32, (rows, columns - width), 1)
    labels = jnp.zeros_like(lane)
    for k in range(topk):
        gate = gate_ref[:, k : k + 1]
        labels = jnp.where(lane == k, route_ref[:, k : k + 1], labels)
        labels = jnp.where(lane == topk + k, lax.shift_right_logical(gate, 8), labels)
        labels = jnp.where(lane == 2 * topk + k, gate & 255, labels)
    labels = labels.astype(jnp.float32).astype(jnp.bfloat16)
    own_ref[:rows, :width] = tok_ref[...]
    own_ref[rows:, :width] = cot_ref[...]
    own_ref[:rows, width:] = labels
    own_ref[rows:, width:] = jnp.zeros_like(labels)

    def slab(z, d):
        return out_ref.at[level[z], spot[d]]

    def send(index, src, dst, peer):
        copies[index] = remote(src, dst, sems, index, peer)
        copies[index].start()

    def arrived(index):
        copies[index].wait_recv()

    greet([along_x, along_y, near, far, sibling])
    keep = pltpu.make_async_copy(own_ref, slab(0, 0), local_sem)
    keep.start()

    def spread(z):
        src = own_ref if z == 0 else slab(z, 0)
        send(x_at + z, src, slab(z, 0), along_x)
        send(y_at + z, src, slab(z, 0), along_y)
        send(sib_at + 4 * z, src, slab(z, 0), sibling)

    def corners(z):
        for d, at, half, peer in ((1, x_at, 0, along_y), (2, y_at, 1, along_x)):
            arrived(at + z)
            part = slab(z, d).at[:, pl.ds(half * middle, columns - middle if half else middle)]
            send(diag_at + 2 * z + half, part, part, peer)
            send(sib_at + 4 * z + d, slab(z, d), slab(z, d), sibling)

    def finish(z):
        for half in range(2):
            arrived(diag_at + 2 * z + half)
        send(sib_at + 4 * z + 3, slab(z, 3), slab(z, 3), sibling)

    send(z_at + 2, own_ref, slab(0, 0), far)
    send(z_at + 1, own_ref, slab(0, 0), near)
    spread(0)
    corners(0)
    arrived(z_at + 1)
    spread(1)
    arrived(z_at + 2)
    send(z_at + 3, slab(2, 0), slab(2, 0), near)
    spread(2)
    finish(0)
    corners(1)
    arrived(z_at + 3)
    spread(3)
    corners(2)
    finish(1)
    corners(3)
    finish(2)
    finish(3)
    for z in range(4):
        for d in range(4):
            arrived(sib_at + 4 * z + d)
    for copy in copies.values():
        copy.wait_send()
    keep.wait()


def gather_all(tokens, cotangent, routes, gates):
    rows, width = tokens.shape
    columns = width + LANES
    experts, groups = lax.axis_size("expert"), lax.axis_size("dp")
    return pl.pallas_call(
        gather_kernel,
        out_shape=jax.ShapeDtypeStruct((experts, groups, 2 * rows, columns), tokens.dtype),
        in_specs=[pl.BlockSpec(memory_space=pltpu.VMEM)] * 4,
        out_specs=pl.BlockSpec(memory_space=pl.ANY),
        scratch_shapes=[
            pltpu.VMEM((2 * rows, columns), tokens.dtype),
            pltpu.SemaphoreType.DMA,
            pltpu.SemaphoreType.DMA((36,)),
            pltpu.SemaphoreType.DMA((36,)),
        ],
        compiler_params=pltpu.CompilerParams(collective_id=0, has_side_effects=True),
    )(tokens, cotangent, routes, gates)


def return_kernel(
    parts_ref, packed_ref, widen_ref, place_ref, out_ref, swapped_ref,
    first, second, second_in, third, third_in, send_sem, recv_sem,
):
    me, group = lax.axis_index("expert"), lax.axis_index("dp")
    experts = second.shape[1]
    sems = (send_sem, recv_sem)
    mates = [group, flip(group, 1), flip(group, 2), flip(flip(group, 2), 1)]
    others = [lax.rem(me + m, experts) for m in range(experts)]
    step = 6 + experts
    copies = {}

    def send(index, src, dst, peer):
        copies[index] = remote(src, dst, sems, index, peer)
        copies[index].start()

    greet([(me, mates[r]) for r in (1, 2, 3)] + [(others[m], group) for m in range(1, experts)])
    send(CHUNKS * step, packed_ref, swapped_ref, (flip(me, experts // 2), group))
    for c in range(CHUNKS):
        for r in (3, 1, 2):
            send(c * step + r, parts_ref.at[mates[r] * CHUNKS + c], first.at[c, r], (me, mates[r]))

    def back(c):
        total = parts_ref[group * CHUNKS + c].astype(jnp.float32)
        for r in (1, 2, 3):
            copies[c * step + r].wait_recv()
            total = total + first[c, r].astype(jnp.float32)
        total = total.astype(jnp.bfloat16)
        for i in range(experts):
            block = jnp.dot(widen_ref[i], total, preferred_element_type=jnp.float32)
            second[c, i] = block.astype(jnp.bfloat16)
        for m in (4, 5, 3, 6, 2, 7, 1):
            send(c * step + 3 + m, second.at[c, others[m]], second_in.at[c, me], (others[m], group))
        second_in[c, me] = second[c, me]

    def join(c):
        for m in range(1, experts):
            copies[c * step + 3 + m].wait_recv()
        total = jnp.zeros((place_ref.shape[1], second.shape[3]), jnp.float32)
        for i in range(experts):
            total = total + jnp.dot(
                place_ref[i], second_in[c, i], preferred_element_type=jnp.float32
            )
        total = total.astype(jnp.bfloat16)
        rows = third.shape[2]
        for r in range(4):
            third[c, r] = total[r * rows : (r + 1) * rows]
        for r in (3, 1, 2):
            send(c * step + 2 + experts + r, third.at[c, mates[r]], third_in.at[c, group], (me, mates[r]))
        third_in[c, group] = third[c, group]

    for c in range(CHUNKS + LAG):
        if c < CHUNKS:
            back(c)
        if c >= LAG:
            join(c - LAG)
    for c in range(CHUNKS):
        for r in (1, 2, 3):
            copies[c * step + 2 + experts + r].wait_recv()
        columns = third.shape[3]
        for r in range(4):
            at = (r * CHUNKS + c) * columns
            out_ref[:, at : at + columns] = third_in[c, r]
    copies[CHUNKS * step].wait_recv()
    for copy in copies.values():
        copy.wait_send()


def return_all(parts, packed, widen, place, rows_out):
    pieces, slots, columns = parts.shape
    experts, wide = widen.shape[:2]
    groups = pieces // CHUNKS
    vmem = pl.BlockSpec(memory_space=pltpu.VMEM)
    count = CHUNKS * (6 + experts) + 1
    return pl.pallas_call(
        return_kernel,
        out_shape=(
            jax.ShapeDtypeStruct((rows_out, pieces * columns), jnp.bfloat16),
            jax.ShapeDtypeStruct(packed.shape, packed.dtype),
        ),
        in_specs=[vmem] * 4,
        out_specs=(vmem, vmem),
        scratch_shapes=[
            pltpu.VMEM((CHUNKS, 4, slots, columns), jnp.bfloat16),
            pltpu.VMEM((CHUNKS, experts, wide, columns), jnp.bfloat16),
            pltpu.VMEM((CHUNKS, experts, wide, columns), jnp.bfloat16),
            pltpu.VMEM((CHUNKS, groups, rows_out, columns), jnp.bfloat16),
            pltpu.VMEM((CHUNKS, groups, rows_out, columns), jnp.bfloat16),
            pltpu.SemaphoreType.DMA((count,)),
            pltpu.SemaphoreType.DMA((count,)),
        ],
        compiler_params=pltpu.CompilerParams(
            collective_id=1, has_side_effects=True, vmem_limit_bytes=48 * 2**20
        ),
    )(parts, packed, widen, place)


def expert_kernel(
    tiles, pick_ref, weight_ref, rows_ref, w_gate_ref, w_up_ref, w_down_ref,
    theirs_ref, packed_ref, parts_ref, gate_acc, up_acc, hidden_acc,
):
    j = pl.program_id(0)
    slots, units = gate_acc.shape

    @pl.when(j == 0)
    def _():
        gate_acc[...] = jnp.zeros_like(gate_acc)
        up_acc[...] = jnp.zeros_like(up_acc)
        hidden_acc[...] = jnp.zeros_like(hidden_acc)

    @pl.when(j < tiles)
    def _():
        rows = rows_ref[...]
        mine = jnp.dot(pick_ref[: 2 * slots], rows, preferred_element_type=jnp.float32)
        theirs = jnp.dot(pick_ref[2 * slots :], rows, preferred_element_type=jnp.float32)
        theirs_ref[...] = theirs.astype(jnp.bfloat16)
        rows_in = mine[:slots].astype(jnp.bfloat16)
        rows_cot = (mine[slots:] * weight_ref[...]).astype(jnp.bfloat16)
        gate_acc[...] += jnp.dot(rows_in, w_gate_ref[...], preferred_element_type=jnp.float32)
        up_acc[...] += jnp.dot(rows_in, w_up_ref[...], preferred_element_type=jnp.float32)
        hidden_acc[...] += contract_units(rows_cot, w_down_ref[...])

    @pl.when(j == tiles - 1)
    def _():
        gate_act, up_act, d_hidden = gate_acc[...], up_acc[...], hidden_acc[...]
        sigmoid_gate = 1.0 / (1.0 + jnp.exp(-gate_act))
        silu = gate_act * sigmoid_gate
        d_gate = d_hidden * up_act * sigmoid_gate * (1.0 + gate_act * (1.0 - sigmoid_gate))
        packed_ref[:, :units] = d_gate.astype(jnp.bfloat16)
        packed_ref[:, units : 2 * units] = (d_hidden * silu).astype(jnp.bfloat16)
        packed_ref[:, 2 * units :] = (silu * up_act * weight_ref[...]).astype(jnp.bfloat16)

    @pl.when(j >= tiles)
    def _():
        d_gate, d_up = packed_ref[:, :units], packed_ref[:, units : 2 * units]
        pieces, _, columns = parts_ref.shape
        for p in range(pieces):
            at = pl.ds(p * columns, columns)
            share = contract_units(d_gate, w_gate_ref[at]) + contract_units(d_up, w_up_ref[at])
            parts_ref[p] = share.astype(jnp.bfloat16)


def expert_all(pick, weight, rows_all, w_gate, w_up, w_down, pieces):
    slots, units = weight.shape[0], w_gate.shape[1]
    width = w_gate.shape[0]
    count = rows_all.shape[0]
    tiles = CHUNKS
    tile = width // tiles
    columns = width // pieces

    def fixed(*shape):
        return pl.BlockSpec(shape, lambda j: (0,) * len(shape))

    def ahead(j):
        return lax.min(j, tiles - 1)

    return pl.pallas_call(
        lambda *refs: expert_kernel(tiles, *refs),
        grid=(2 * tiles,),
        out_shape=(
            jax.ShapeDtypeStruct((2 * slots, width), jnp.bfloat16),
            jax.ShapeDtypeStruct((slots, 3 * units), jnp.bfloat16),
            jax.ShapeDtypeStruct((pieces, slots, columns), jnp.bfloat16),
        ),
        in_specs=[
            fixed(*pick.shape),
            fixed(slots, 1),
            pl.BlockSpec((count, tile), lambda j: (0, ahead(j))),
            pl.BlockSpec((tile, units), lambda j: (lax.rem(j, tiles), 0)),
            pl.BlockSpec((tile, units), lambda j: (lax.rem(j, tiles), 0)),
            pl.BlockSpec((units, tile), lambda j: (0, ahead(j))),
        ],
        out_specs=(
            pl.BlockSpec((2 * slots, tile), lambda j: (0, ahead(j))),
            fixed(slots, 3 * units),
            pl.BlockSpec(
                (pieces // tiles, slots, columns), lambda j: (lax.max(j - tiles, 0), 0, 0)
            ),
        ),
        scratch_shapes=[pltpu.VMEM((slots, units), jnp.float32)] * 3,
        compiler_params=pltpu.CompilerParams(vmem_limit_bytes=40 * 2**20),
    )(pick, weight, rows_all, w_gate, w_up, w_down)


def small_shards(tokens, cotangent, w_gate, w_up, w_down, routes, gates, matching):
    rows_here, width = tokens.shape[2:]
    topk = routes.shape[3]
    units = w_gate.shape[2]
    expert_count = lax.axis_size("expert")
    group_count = lax.axis_size("dp")
    column_tok = group_count * rows_here
    cap_col = 3 * group_count * rows_here * topk // (2 * expert_count)
    slot_count = expert_count * cap_col
    self_index = lax.axis_index("expert")
    expert_iota = jnp.arange(expert_count, dtype=jnp.int32)
    partner = jnp.sum(jnp.where(expert_iota == self_index, matching, 0))
    flipped = partner != self_index
    everything = gather_all(tokens[0, 0], cotangent[0, 0], routes[0, 0], gates[0, 0])
    labels = everything[:, :, :rows_here, width : width + 3 * topk].astype(jnp.int32)
    labels = labels.reshape(expert_count, column_tok, 3, topk)
    route = labels[:, :, 0]
    gate = labels[:, :, 1] * 256 + labels[:, :, 2]
    rows_all = everything.reshape(expert_count * group_count * 2 * rows_here, width + LANES)

    def ranked(expert):
        hit = jnp.any(route == expert, axis=2)
        at = jnp.arange(column_tok, dtype=jnp.int32)
        before = (at[None, :] < at[:, None])[None] & hit[:, None, :]
        ranking = jnp.sum(before, axis=2, dtype=jnp.int32)
        slot = expert_iota[:, None] * cap_col + ranking
        return jnp.where(hit, slot, -1).reshape(expert_count, group_count, rows_here)

    def picked(expert):
        slot = ranked(expert)
        none = jnp.full_like(slot, -1)
        from_tok = jnp.concatenate([slot, none], axis=2).reshape(-1)
        from_cot = jnp.concatenate([none, slot], axis=2).reshape(-1)
        iota = jnp.arange(slot_count, dtype=jnp.int32)[:, None]
        pick = jnp.concatenate([from_tok[None] == iota, from_cot[None] == iota], axis=0)
        return pick.astype(jnp.bfloat16)

    weight = jnp.sum(jnp.where(route == self_index, gate, 0), axis=2).reshape(-1)
    own_slot = ranked(self_index).reshape(-1)
    slot_iota = jnp.arange(slot_count, dtype=jnp.int32)[:, None]
    weight = jnp.sum(jnp.where(own_slot[None] == slot_iota, weight[None], 0), axis=1)
    weight = (weight.astype(jnp.float32) / 65536.0)[:, None]
    pick = jnp.concatenate([picked(self_index), picked(partner)], axis=0)
    pieces = group_count * CHUNKS
    theirs, packed, parts = expert_all(
        pick, weight, rows_all, w_gate[0], w_up[0], w_down[0], pieces
    )
    wide = -(-cap_col // ROW_TILE) * ROW_TILE
    widen = np.zeros((expert_count, wide, slot_count), np.float32)
    for i in range(expert_count):
        widen[i, np.arange(cap_col), i * cap_col + np.arange(cap_col)] = 1.0
    column_route = jnp.sum(
        jnp.where(expert_iota[:, None, None] == self_index, route, 0), axis=0
    )
    hits = jnp.any(column_route[None] == expert_iota[:, None, None], axis=2)
    at = jnp.arange(column_tok, dtype=jnp.int32)
    ranking = jnp.sum(
        (at[None, :] < at[:, None])[None] & hits[:, None, :], axis=2, dtype=jnp.int32
    )
    place = (ranking[:, :, None] == jnp.arange(wide)[None, None]) & hits[:, :, None]
    rows_out = -(-rows_here // 16) * 16
    place = place.reshape(expert_count, group_count, rows_here, wide)
    place = jnp.pad(place, ((0, 0), (0, 0), (0, rows_out - rows_here), (0, 0)))
    place = place.reshape(expert_count, group_count * rows_out, wide).astype(jnp.bfloat16)
    total, swapped = return_all(
        parts, packed, jnp.asarray(widen, jnp.bfloat16), place, rows_out
    )
    chosen = jnp.where(flipped, swapped, packed)
    their_rows, their_cot = theirs[:slot_count], theirs[slot_count:]
    grad_gate = contract_rows(their_rows, chosen[:, :units]).astype(jnp.bfloat16)
    grad_up = contract_rows(their_rows, chosen[:, units : 2 * units]).astype(jnp.bfloat16)
    grad_down = contract_rows(chosen[:, 2 * units :], their_cot).astype(jnp.bfloat16)
    return (
        total[:rows_here].reshape(1, 1, rows_here, width),
        grad_gate[None],
        grad_up[None],
        grad_down[None],
    )


def step(tokens, *rest):
    small = lax.axis_size("expert") == 8 and lax.axis_size("dp") == 4
    return (small_shards if small else shards)(tokens, *rest)


def solution(mesh):
    placed = (
        P("expert", "dp", None, None),
        P("expert", "dp", None, None),
        P("expert", None, "dp"),
        P("expert", None, "dp"),
        P("expert", "dp", None),
        P("expert", "dp", None, None),
        P("expert", "dp", None, None),
        P(),
    )
    return jax.shard_map(
        step,
        mesh=mesh,
        in_specs=placed,
        out_specs=(
            P("expert", "dp", None, None),
            P("expert", None, "dp"),
            P("expert", None, "dp"),
            P("expert", "dp", None),
        ),
        check_vma=False,
    )
```

```python
import jax
import jax.numpy as jnp
import numpy as np
from jax import lax
from jax.experimental import pallas as pl
from jax.experimental.pallas import tpu as pltpu
from jax.sharding import PartitionSpec as P

MESH = pl.DeviceIdType.MESH
LANES = 128
ROW_TILE = 8
CHUNKS = 7
LAG = 2


def from_partner(x, axis, distance):
    return lax.ppermute(x, axis, [(i, i ^ 1 << distance) for i in range(lax.axis_size(axis))])


def column_places(route_flat, owner_table, expert_count, cap_col):
    choices_iota = jnp.arange(expert_count, dtype=jnp.int32)
    onehot = (route_flat[:, None] == choices_iota[None, :]).astype(jnp.int32)
    ranking = jnp.sum(jnp.cumsum(onehot, axis=0) * onehot, axis=1) - 1
    target = jnp.sum(onehot * owner_table[None, :], axis=1)
    position = target * cap_col + ranking
    slot_iota = jnp.arange(expert_count * cap_col, dtype=jnp.int32)
    return slot_iota[:, None] == position[None, :]


def contract_rows(left, right):
    return lax.dot_general(
        left, right, (((0,), (0,)), ((), ())), preferred_element_type=jnp.float32
    )


def contract_units(left, right):
    return lax.dot_general(
        left, right, (((1,), (1,)), ((), ())), preferred_element_type=jnp.float32
    )


def shards(tokens, cotangent, w_gate, w_up, w_down, routes, gates, matching):
    rows_here = tokens.shape[2]
    width = tokens.shape[3]
    topk = routes.shape[3]
    expert_count = lax.axis_size("expert")
    group_count = lax.axis_size("dp")
    cap_col = 3 * group_count * rows_here * topk // (2 * expert_count)
    slot_count = expert_count * cap_col
    column_tok = group_count * rows_here
    self_index = lax.axis_index("expert")
    pair_bit = expert_count.bit_length() - 2
    expert_iota = jnp.arange(expert_count, dtype=jnp.int32)
    partner = jnp.sum(jnp.where(expert_iota == self_index, matching, 0))
    flipped = partner != self_index
    weight_gate = w_gate[0]
    weight_up = w_up[0]
    weight_down = w_down[0]
    swapped = from_partner((weight_gate, weight_up, weight_down), "expert", pair_bit)
    weight_gate = jnp.where(flipped, swapped[0], weight_gate)
    weight_up = jnp.where(flipped, swapped[1], weight_up)
    weight_down = jnp.where(flipped, swapped[2], weight_down)
    labels = (
        lax.all_gather(routes, "dp", axis=1, tiled=True),
        lax.all_gather(gates, "dp", axis=1, tiled=True),
    )
    route_col = labels[0].reshape(column_tok * topk)
    gate_col = labels[1].reshape(column_tok, topk).astype(jnp.float32) / 65536.0
    places = column_places(route_col, matching, expert_count, cap_col)
    place_pick = places.astype(jnp.bfloat16)
    place_tok = jnp.any(places.reshape(slot_count, column_tok, topk), axis=2).astype(jnp.bfloat16)
    column = (
        lax.all_gather(tokens, "dp", axis=1, tiled=True),
        lax.all_gather(cotangent, "dp", axis=1, tiled=True),
    )
    col_in = column[0].reshape(column_tok, width)
    col_cot = column[1].reshape(column_tok, width)
    send_in = jnp.dot(place_tok, col_in, preferred_element_type=jnp.float32).astype(jnp.bfloat16)
    dy_pick = (gate_col[:, :, None] * col_cot[:, None, :].astype(jnp.float32)).astype(jnp.bfloat16)
    send_cot = jnp.dot(
        place_pick, dy_pick.reshape(column_tok * topk, width), preferred_element_type=jnp.float32
    ).astype(jnp.bfloat16)
    arrived = (
        lax.all_to_all(
            send_in.reshape(expert_count, cap_col, width),
            "expert",
            split_axis=0,
            concat_axis=0,
            tiled=True,
        ),
        lax.all_to_all(
            send_cot.reshape(expert_count, cap_col, width),
            "expert",
            split_axis=0,
            concat_axis=0,
            tiled=True,
        ),
    )
    routed_rows = arrived[0].reshape(slot_count, width)
    routed_cot = arrived[1].reshape(slot_count, width)
    gate_act = jnp.dot(routed_rows, weight_gate, preferred_element_type=jnp.float32)
    up_act = jnp.dot(routed_rows, weight_up, preferred_element_type=jnp.float32)
    sigmoid_gate = jax.nn.sigmoid(gate_act)
    hidden = (gate_act * sigmoid_gate * up_act).astype(jnp.bfloat16)
    grad_down_here = contract_rows(hidden, routed_cot).astype(jnp.bfloat16)
    d_hidden = contract_units(routed_cot, weight_down)
    d_gate = (d_hidden * up_act * sigmoid_gate * (1.0 + gate_act * (1.0 - sigmoid_gate))).astype(
        jnp.bfloat16
    )
    d_up = (d_hidden * gate_act * sigmoid_gate).astype(jnp.bfloat16)
    grad_gate_here = contract_rows(routed_rows, d_gate).astype(jnp.bfloat16)
    grad_up_here = contract_rows(routed_rows, d_up).astype(jnp.bfloat16)
    partial_terms = contract_units(d_gate, weight_gate) + contract_units(d_up, weight_up)
    parts = partial_terms.astype(jnp.bfloat16).reshape(expert_count, cap_col, width)
    back = lax.all_to_all(parts, "expert", split_axis=0, concat_axis=0, tiled=True)
    col_sum = contract_rows(place_tok, back.reshape(slot_count, width))
    total = lax.psum_scatter(
        col_sum.reshape(group_count, rows_here, width).astype(jnp.bfloat16),
        "dp",
        scatter_dimension=0,
        tiled=True,
    )
    return (
        total.reshape(1, 1, rows_here, width),
        grad_gate_here[None],
        grad_up_here[None],
        grad_down_here[None],
    )


def flip(index, bit):
    return index + bit - 2 * bit * lax.rem(lax.div(index, bit), 2)


def greet(peers):
    barrier = pltpu.get_barrier_semaphore()
    for peer in peers:
        place = {"expert": peer[0], "dp": peer[1]}
        pl.semaphore_signal(barrier, inc=1, device_id=place, device_id_type=MESH)
    pl.semaphore_wait(barrier, len(peers))


def remote(src, dst, sems, index, peer):
    return pltpu.make_async_remote_copy(
        src_ref=src,
        dst_ref=dst,
        send_sem=sems[0].at[index],
        recv_sem=sems[1].at[index],
        device_id={"expert": peer[0], "dp": peer[1]},
        device_id_type=MESH,
    )


def gather_kernel(
    tok_ref, cot_ref, label_ref, out_ref, own_ref, local_sem, send_sem, recv_sem
):
    me, group = lax.axis_index("expert"), lax.axis_index("dp")
    sems = (send_sem, recv_sem)
    along_x, along_y = (me, flip(group, 1)), (me, flip(group, 2))
    near, far, sibling = (flip(me, 2), group), (flip(me, 4), group), (flip(me, 1), group)
    level = [me, flip(me, 2), flip(me, 4), flip(flip(me, 4), 2)]
    spot = [group, flip(group, 1), flip(group, 2), flip(flip(group, 2), 1)]
    z_at, x_at, y_at, diag_at, sib_at = 0, 4, 8, 12, 20
    copies = {}
    rows, width = tok_ref.shape
    columns = out_ref.shape[3]
    middle = width // 2
    topk = label_ref.shape[1] // 2
    lane = lax.broadcasted_iota(jnp.int32, (rows, columns - width), 1)
    labels = jnp.zeros_like(lane)
    for k in range(topk):
        gate = label_ref[:, topk + k : topk + k + 1]
        labels = jnp.where(lane == k, label_ref[:, k : k + 1], labels)
        labels = jnp.where(lane == topk + k, lax.shift_right_logical(gate, 8), labels)
        labels = jnp.where(lane == 2 * topk + k, gate & 255, labels)
    labels = labels.astype(jnp.float32).astype(jnp.bfloat16)
    own_ref[:rows, :width] = tok_ref[...]
    own_ref[rows:, :width] = cot_ref[...]
    own_ref[:rows, width:] = labels
    own_ref[rows:, width:] = jnp.zeros_like(labels)

    def slab(z, d):
        return out_ref.at[level[z], spot[d]]

    def send(index, src, dst, peer):
        copies[index] = remote(src, dst, sems, index, peer)
        copies[index].start()

    def arrived(index):
        copies[index].wait_recv()

    greet([along_x, along_y, near, far, sibling])
    keep = pltpu.make_async_copy(own_ref, slab(0, 0), local_sem)
    keep.start()

    def spread(z):
        src = own_ref if z == 0 else slab(z, 0)
        send(x_at + z, src, slab(z, 0), along_x)
        send(y_at + z, src, slab(z, 0), along_y)
        send(sib_at + 4 * z, src, slab(z, 0), sibling)

    def corners(z):
        for d, at, half, peer in ((1, x_at, 0, along_y), (2, y_at, 1, along_x)):
            arrived(at + z)
            part = slab(z, d).at[:, pl.ds(half * middle, columns - middle if half else middle)]
            send(diag_at + 2 * z + half, part, part, peer)
            send(sib_at + 4 * z + d, slab(z, d), slab(z, d), sibling)

    def finish(z):
        for half in range(2):
            arrived(diag_at + 2 * z + half)
        send(sib_at + 4 * z + 3, slab(z, 3), slab(z, 3), sibling)

    send(z_at + 2, own_ref, slab(0, 0), far)
    send(z_at + 1, own_ref, slab(0, 0), near)
    spread(0)
    corners(0)
    arrived(z_at + 1)
    spread(1)
    arrived(z_at + 2)
    send(z_at + 3, slab(2, 0), slab(2, 0), near)
    spread(2)
    finish(0)
    corners(1)
    arrived(z_at + 3)
    spread(3)
    corners(2)
    finish(1)
    corners(3)
    finish(2)
    finish(3)
    for z in range(4):
        for d in range(4):
            arrived(sib_at + 4 * z + d)
    for copy in copies.values():
        copy.wait_send()
    keep.wait()


def gather_all(tokens, cotangent, labels):
    rows, width = tokens.shape
    columns = width + LANES
    experts, groups = lax.axis_size("expert"), lax.axis_size("dp")
    return pl.pallas_call(
        gather_kernel,
        out_shape=jax.ShapeDtypeStruct((experts, groups, 2 * rows, columns), tokens.dtype),
        in_specs=[pl.BlockSpec(memory_space=pltpu.VMEM)] * 3,
        out_specs=pl.BlockSpec(memory_space=pl.ANY),
        scratch_shapes=[
            pltpu.VMEM((2 * rows, columns), tokens.dtype),
            pltpu.SemaphoreType.DMA,
            pltpu.SemaphoreType.DMA((36,)),
            pltpu.SemaphoreType.DMA((36,)),
        ],
        compiler_params=pltpu.CompilerParams(collective_id=0, has_side_effects=True),
    )(tokens, cotangent, labels)


def return_kernel(
    parts_ref, packed_ref, widen_ref, place_ref, pick_ref, rows_ref, out_ref, swapped_ref,
    theirs_ref, first, second, second_in, third, third_in, held, send_sem, recv_sem, tile_sem,
):
    me, group = lax.axis_index("expert"), lax.axis_index("dp")
    experts = second.shape[1]
    sems = (send_sem, recv_sem)
    mates = [group, flip(group, 1), flip(group, 2), flip(flip(group, 2), 1)]
    others = [lax.rem(me + m, experts) for m in range(experts)]
    step = 6 + experts
    copies = {}

    def send(index, src, dst, peer):
        copies[index] = remote(src, dst, sems, index, peer)
        copies[index].start()

    tile = held.shape[2]

    def fetch(c):
        source = rows_ref.at[:, pl.ds(c * tile, tile)]
        return pltpu.make_async_copy(source, held.at[c % 2], tile_sem.at[c % 2])

    def pick(c):
        fetch(c).wait()
        if c + 1 < CHUNKS:
            fetch(c + 1).start()
        rows = jnp.dot(pick_ref[...], held[c % 2], preferred_element_type=jnp.float32)
        theirs_ref[:, c * tile : (c + 1) * tile] = rows.astype(jnp.bfloat16)

    fetch(0).start()
    greet([(me, mates[r]) for r in (1, 2, 3)] + [(others[m], group) for m in range(1, experts)])
    send(CHUNKS * step, packed_ref, swapped_ref, (flip(me, experts // 2), group))
    for c in range(CHUNKS):
        for r in (3, 1, 2):
            send(c * step + r, parts_ref.at[mates[r] * CHUNKS + c], first.at[c, r], (me, mates[r]))

    def back(c):
        total = parts_ref[group * CHUNKS + c].astype(jnp.float32)
        for r in (1, 2, 3):
            copies[c * step + r].wait_recv()
            total = total + first[c, r].astype(jnp.float32)
        total = total.astype(jnp.bfloat16)
        for i in range(experts):
            block = jnp.dot(widen_ref[i], total, preferred_element_type=jnp.float32)
            second[c, i] = block.astype(jnp.bfloat16)
        for m in (4, 5, 3, 6, 2, 7, 1):
            send(c * step + 3 + m, second.at[c, others[m]], second_in.at[c, me], (others[m], group))
        second_in[c, me] = second[c, me]

    def join(c):
        for m in range(1, experts):
            copies[c * step + 3 + m].wait_recv()
        total = jnp.zeros((place_ref.shape[1], second.shape[3]), jnp.float32)
        for i in range(experts):
            total = total + jnp.dot(
                place_ref[i], second_in[c, i], preferred_element_type=jnp.float32
            )
        total = total.astype(jnp.bfloat16)
        rows = third.shape[2]
        for r in range(4):
            third[c, r] = total[r * rows : (r + 1) * rows]
        for r in (3, 1, 2):
            send(c * step + 2 + experts + r, third.at[c, mates[r]], third_in.at[c, group], (me, mates[r]))
        third_in[c, group] = third[c, group]

    for c in range(CHUNKS + LAG):
        if c < CHUNKS:
            pick(c)
            back(c)
        if c >= LAG:
            join(c - LAG)
    for c in range(CHUNKS):
        for r in (1, 2, 3):
            copies[c * step + 2 + experts + r].wait_recv()
        columns = third.shape[3]
        for r in range(4):
            at = (r * CHUNKS + c) * columns
            out_ref[:, at : at + columns] = third_in[c, r]
    copies[CHUNKS * step].wait_recv()
    for copy in copies.values():
        copy.wait_send()


def return_all(parts, packed, widen, place, pick, rows_all, rows_out):
    pieces, slots, columns = parts.shape
    experts, wide = widen.shape[:2]
    groups = pieces // CHUNKS
    vmem = pl.BlockSpec(memory_space=pltpu.VMEM)
    count = CHUNKS * (6 + experts) + 1
    return pl.pallas_call(
        return_kernel,
        out_shape=(
            jax.ShapeDtypeStruct((rows_out, pieces * columns), jnp.bfloat16),
            jax.ShapeDtypeStruct(packed.shape, packed.dtype),
            jax.ShapeDtypeStruct((pick.shape[0], pieces * columns), jnp.bfloat16),
        ),
        in_specs=[vmem] * 5 + [pl.BlockSpec(memory_space=pl.ANY)],
        out_specs=(vmem, vmem, vmem),
        scratch_shapes=[
            pltpu.VMEM((CHUNKS, 4, slots, columns), jnp.bfloat16),
            pltpu.VMEM((CHUNKS, experts, wide, columns), jnp.bfloat16),
            pltpu.VMEM((CHUNKS, experts, wide, columns), jnp.bfloat16),
            pltpu.VMEM((CHUNKS, groups, rows_out, columns), jnp.bfloat16),
            pltpu.VMEM((CHUNKS, groups, rows_out, columns), jnp.bfloat16),
            pltpu.VMEM((2, rows_all.shape[0], pieces * columns // CHUNKS), jnp.bfloat16),
            pltpu.SemaphoreType.DMA((count,)),
            pltpu.SemaphoreType.DMA((count,)),
            pltpu.SemaphoreType.DMA((2,)),
        ],
        compiler_params=pltpu.CompilerParams(
            collective_id=1, has_side_effects=True, vmem_limit_bytes=60 * 2**20
        ),
    )(parts, packed, widen, place, pick, rows_all)


def expert_kernel(
    tiles, pick_ref, weight_ref, rows_ref, w_gate_ref, w_up_ref, w_down_ref,
    packed_ref, parts_ref, gate_acc, up_acc, hidden_acc,
):
    j = pl.program_id(0)
    slots, units = gate_acc.shape

    @pl.when(j == 0)
    def _():
        gate_acc[...] = jnp.zeros_like(gate_acc)
        up_acc[...] = jnp.zeros_like(up_acc)
        hidden_acc[...] = jnp.zeros_like(hidden_acc)

    @pl.when(j < tiles)
    def _():
        rows = rows_ref[...]
        mine = jnp.dot(pick_ref[...], rows, preferred_element_type=jnp.float32)
        rows_in = mine[:slots].astype(jnp.bfloat16)
        rows_cot = (mine[slots:] * weight_ref[...]).astype(jnp.bfloat16)
        gate_acc[...] += jnp.dot(rows_in, w_gate_ref[...], preferred_element_type=jnp.float32)
        up_acc[...] += jnp.dot(rows_in, w_up_ref[...], preferred_element_type=jnp.float32)
        hidden_acc[...] += contract_units(rows_cot, w_down_ref[...])

    @pl.when(j == tiles - 1)
    def _():
        gate_act, up_act, d_hidden = gate_acc[...], up_acc[...], hidden_acc[...]
        sigmoid_gate = 1.0 / (1.0 + jnp.exp(-gate_act))
        silu = gate_act * sigmoid_gate
        d_gate = d_hidden * up_act * sigmoid_gate * (1.0 + gate_act * (1.0 - sigmoid_gate))
        packed_ref[:, :units] = d_gate.astype(jnp.bfloat16)
        packed_ref[:, units : 2 * units] = (d_hidden * silu).astype(jnp.bfloat16)
        packed_ref[:, 2 * units :] = (silu * up_act * weight_ref[...]).astype(jnp.bfloat16)

    @pl.when(j >= tiles)
    def _():
        d_gate, d_up = packed_ref[:, :units], packed_ref[:, units : 2 * units]
        pieces, _, columns = parts_ref.shape
        for p in range(pieces):
            at = pl.ds(p * columns, columns)
            share = contract_units(d_gate, w_gate_ref[at]) + contract_units(d_up, w_up_ref[at])
            parts_ref[p] = share.astype(jnp.bfloat16)


def expert_all(pick, weight, rows_all, w_gate, w_up, w_down, pieces):
    slots, units = weight.shape[0], w_gate.shape[1]
    width = w_gate.shape[0]
    count = rows_all.shape[0]
    tiles = CHUNKS
    tile = width // tiles
    columns = width // pieces

    def fixed(*shape):
        return pl.BlockSpec(shape, lambda j: (0,) * len(shape))

    def ahead(j):
        return lax.min(j, tiles - 1)

    return pl.pallas_call(
        lambda *refs: expert_kernel(tiles, *refs),
        grid=(2 * tiles,),
        out_shape=(
            jax.ShapeDtypeStruct((slots, 3 * units), jnp.bfloat16),
            jax.ShapeDtypeStruct((pieces, slots, columns), jnp.bfloat16),
        ),
        in_specs=[
            fixed(*pick.shape),
            fixed(slots, 1),
            pl.BlockSpec((count, tile), lambda j: (0, ahead(j))),
            pl.BlockSpec((tile, units), lambda j: (lax.rem(j, tiles), 0)),
            pl.BlockSpec((tile, units), lambda j: (lax.rem(j, tiles), 0)),
            pl.BlockSpec((units, tile), lambda j: (0, ahead(j))),
        ],
        out_specs=(
            fixed(slots, 3 * units),
            pl.BlockSpec(
                (pieces // tiles, slots, columns), lambda j: (lax.max(j - tiles, 0), 0, 0)
            ),
        ),
        scratch_shapes=[pltpu.VMEM((slots, units), jnp.float32)] * 3,
        compiler_params=pltpu.CompilerParams(vmem_limit_bytes=60 * 2**20),
    )(pick, weight, rows_all, w_gate, w_up, w_down)


def small_shards(tokens, cotangent, w_gate, w_up, w_down, routes, gates, matching):
    rows_here, width = tokens.shape[2:]
    topk = routes.shape[3]
    units = w_gate.shape[2]
    expert_count = lax.axis_size("expert")
    group_count = lax.axis_size("dp")
    column_tok = group_count * rows_here
    cap_col = 3 * group_count * rows_here * topk // (2 * expert_count)
    slot_count = expert_count * cap_col
    self_index = lax.axis_index("expert")
    expert_iota = jnp.arange(expert_count, dtype=jnp.int32)
    partner = jnp.sum(jnp.where(expert_iota == self_index, matching, 0))
    flipped = partner != self_index
    labels = jnp.concatenate([routes[0, 0], gates[0, 0]], axis=1)
    everything = gather_all(tokens[0, 0], cotangent[0, 0], labels)
    labels = everything[:, :, :rows_here, width : width + 3 * topk].astype(jnp.int32)
    labels = labels.reshape(expert_count, column_tok, 3, topk)
    route = labels[:, :, 0]
    gate = labels[:, :, 1] * 256 + labels[:, :, 2]
    rows_all = everything.reshape(expert_count * group_count * 2 * rows_here, width + LANES)

    def ranked(expert):
        hit = jnp.any(route == expert, axis=2)
        at = jnp.arange(column_tok, dtype=jnp.int32)
        before = (at[None, :] < at[:, None])[None] & hit[:, None, :]
        ranking = jnp.sum(before, axis=2, dtype=jnp.int32)
        slot = expert_iota[:, None] * cap_col + ranking
        return jnp.where(hit, slot, -1).reshape(expert_count, group_count, rows_here)

    def picked(expert):
        slot = ranked(expert)
        none = jnp.full_like(slot, -1)
        from_tok = jnp.concatenate([slot, none], axis=2).reshape(-1)
        from_cot = jnp.concatenate([none, slot], axis=2).reshape(-1)
        iota = jnp.arange(slot_count, dtype=jnp.int32)[:, None]
        pick = jnp.concatenate([from_tok[None] == iota, from_cot[None] == iota], axis=0)
        return pick.astype(jnp.bfloat16)

    weight = jnp.sum(jnp.where(route == self_index, gate, 0), axis=2).reshape(-1)
    own_slot = ranked(self_index).reshape(-1)
    slot_iota = jnp.arange(slot_count, dtype=jnp.int32)[:, None]
    weight = jnp.sum(jnp.where(own_slot[None] == slot_iota, weight[None], 0), axis=1)
    weight = (weight.astype(jnp.float32) / 65536.0)[:, None]
    pieces = group_count * CHUNKS
    packed, parts = expert_all(
        picked(self_index), weight, rows_all, w_gate[0], w_up[0], w_down[0], pieces
    )
    wide = -(-cap_col // ROW_TILE) * ROW_TILE
    widen = np.zeros((expert_count, wide, slot_count), np.float32)
    for i in range(expert_count):
        widen[i, np.arange(cap_col), i * cap_col + np.arange(cap_col)] = 1.0
    column_route = jnp.sum(
        jnp.where(expert_iota[:, None, None] == self_index, route, 0), axis=0
    )
    hits = jnp.any(column_route[None] == expert_iota[:, None, None], axis=2)
    at = jnp.arange(column_tok, dtype=jnp.int32)
    ranking = jnp.sum(
        (at[None, :] < at[:, None])[None] & hits[:, None, :], axis=2, dtype=jnp.int32
    )
    place = (ranking[:, :, None] == jnp.arange(wide)[None, None]) & hits[:, :, None]
    rows_out = -(-rows_here // 16) * 16
    place = place.reshape(expert_count, group_count, rows_here, wide)
    place = jnp.pad(place, ((0, 0), (0, 0), (0, rows_out - rows_here), (0, 0)))
    place = place.reshape(expert_count, group_count * rows_out, wide).astype(jnp.bfloat16)
    widen = jnp.asarray(widen, jnp.bfloat16)
    total, swapped, theirs = return_all(
        parts, packed, widen, place, picked(partner), rows_all, rows_out
    )
    chosen = jnp.where(flipped, swapped, packed)
    their_rows, their_cot = theirs[:slot_count], theirs[slot_count:]
    grad_gate = contract_rows(their_rows, chosen[:, :units]).astype(jnp.bfloat16)
    grad_up = contract_rows(their_rows, chosen[:, units : 2 * units]).astype(jnp.bfloat16)
    grad_down = contract_rows(chosen[:, 2 * units :], their_cot).astype(jnp.bfloat16)
    return (
        total[:rows_here].reshape(1, 1, rows_here, width),
        grad_gate[None],
        grad_up[None],
        grad_down[None],
    )


def step(tokens, *rest):
    small = lax.axis_size("expert") == 8 and lax.axis_size("dp") == 4
    return (small_shards if small else shards)(tokens, *rest)


def solution(mesh):
    placed = (
        P("expert", "dp", None, None),
        P("expert", "dp", None, None),
        P("expert", None, "dp"),
        P("expert", None, "dp"),
        P("expert", "dp", None),
        P("expert", "dp", None, None),
        P("expert", "dp", None, None),
        P(),
    )
    return jax.shard_map(
        step,
        mesh=mesh,
        in_specs=placed,
        out_specs=(
            P("expert", "dp", None, None),
            P("expert", None, "dp"),
            P("expert", None, "dp"),
            P("expert", "dp", None),
        ),
        check_vma=False,
    )
```
